256 devices in a mesh: seq: 32 (over x, z), head: 8 (over y, core).
Axes of the slice: x: 4, y: 4, z: 8, core: 2. Of those that a mesh axis runs over, the one named last changes fastest.
Arguments:
- queries: bfloat16 [65536, 4096], P('seq', 'head'), may hold values from -64 to 64
- keys: bfloat16 [65536, 1024], P('seq', 'head'), may hold values from -13 to 13
- values: bfloat16 [65536, 1024], P('seq', 'head'), may hold values from -18 to 18
- assignments: int32 [8, 65536], P('head', 'seq'), may hold values from 0 to 511, as said below
- norm_gain: float32 [4096], P('head'), may hold values from 0.5 to 1.5
Outputs:
- normed: bfloat16 [65536, 4096], P('seq', 'head')
The draws below stay inside these ranges and needn't reach their ends.
Inputs may be any that keep to these rules, and one draw needn't show every extreme that they name: `assignments`: every code is assigned to one or more tokens of each key head.
All inputs are finite; a program needn't handle non-finite values.
Results may differ from the reference program's by a relative error of at most 0.0074.
Values may be sent and summed in bfloat16 or wider, within the bound.
No kernel may reach another device: no remote copies, remote signals or barrier semaphores. Data moves between devices by JAX's collectives and lax.ppermute only.
A program may use at most 128 MiB of HBM per device.

```python
import math
import jax
import jax.numpy as jnp
from jax import lax

DH = 128
QH = 32
KH = 8
CODES = 512
BLK = 256
TOKENS = 65536


def centers_table(key):
    raw = jax.random.normal(jax.random.fold_in(key, 101), (KH, CODES, DH), jnp.float32) * 2.0
    return jnp.clip(raw, -8.0, 8.0)


def code_table(key):
    table = jax.random.randint(jax.random.fold_in(key, 202), (KH, TOKENS), 0, CODES, dtype=jnp.int32)
    stride = TOKENS // CODES
    spots = jnp.arange(CODES, dtype=jnp.int32) * stride
    fixed = jnp.broadcast_to(jnp.arange(CODES, dtype=jnp.int32), (KH, CODES))
    return table.at[:, spots].set(fixed)


def member_centers(key):
    centers = centers_table(key)
    table = code_table(key)
    picked = jax.vmap(lambda rows, picks: jnp.take(rows, picks, axis=0))(centers, table)
    return jnp.transpose(picked, (1, 0, 2))


def draw_assignments(key, part):
    table = code_table(key)
    return table


def draw_keys(key, part):
    base = member_centers(key).reshape(TOKENS, KH * DH)
    key = jax.random.fold_in(key, 2)
    noise = jnp.clip(jax.random.normal(key, (TOKENS, KH * DH), jnp.float32), -5.0, 5.0)
    return (base + noise).astype(jnp.bfloat16)


def draw_queries(key, part):
    key = jax.random.fold_in(key, 3)
    result = jnp.clip(jax.random.normal(key, (TOKENS, QH * DH), jnp.float32), -6.0, 6.0)
    return result.astype(jnp.bfloat16)


def draw_values(key, part):
    key = jax.random.fold_in(key, 4)
    head_scale = 3.0 ** (jnp.arange(KH, dtype=jnp.float32) / (KH - 1))
    raw = jnp.clip(jax.random.normal(key, (TOKENS, KH, DH), jnp.float32), -6.0, 6.0)
    return (raw * head_scale[None, :, None]).reshape(TOKENS, KH * DH).astype(jnp.bfloat16)


def setup_inputs(seed: int = 0) -> dict:
    arg_keys = jax.random.split(jax.random.key(seed), 6)
    queries = draw_queries(jax.random.fold_in(arg_keys[5], 71), 0)
    keys = draw_keys(jax.random.fold_in(arg_keys[5], 71), 0)
    values = draw_values(jax.random.fold_in(arg_keys[5], 71), 0)
    assignments = draw_assignments(jax.random.fold_in(arg_keys[5], 71), 0)
    norm_gain = jnp.clip(1.0 + 0.1 * jax.random.normal(arg_keys[4], (QH * DH,), jnp.float32), 0.5, 1.5)
    return dict(queries=queries, keys=keys, values=values, assignments=assignments, norm_gain=norm_gain)


def attend_block(query_rows, cur_keys, cur_values, prev_keys, prev_values, cache_values, cache_counts, codes, has_prev):
    scale = 1.0 / math.sqrt(DH)
    query_f = query_rows.astype(jnp.float32)
    code_scores = jnp.einsum('thgd,hcd->hgtc', query_f, codes.astype(jnp.float32)) * scale
    prev_scores = jnp.einsum('thgd,hjd->hgtj', query_f, prev_keys.astype(jnp.float32)) * scale
    cur_scores = jnp.einsum('thgd,hjd->hgtj', query_f, cur_keys.astype(jnp.float32)) * scale
    width = cur_keys.shape[1]
    causal = jnp.arange(width, dtype=jnp.int32)[:, None] >= jnp.arange(width, dtype=jnp.int32)[None, :]
    valid = (cache_counts > 0.0)[:, None, None, :]
    lowest = jnp.asarray(-jnp.inf, jnp.float32)
    top = jnp.maximum(lax.optimization_barrier(jnp.max(jnp.where(valid, code_scores, lowest), axis=-1)), lax.optimization_barrier(jnp.max(jnp.where(causal, cur_scores, lowest), axis=-1)))
    top = jnp.maximum(top, jnp.where(has_prev > 0.0, lax.optimization_barrier(jnp.max(prev_scores, axis=-1)), lowest))
    code_weights = jnp.where(valid, jnp.exp(code_scores - top[..., None]), 0.0)
    prev_weights = jnp.exp(prev_scores - top[..., None]) * has_prev
    cur_weights = jnp.where(causal, jnp.exp(cur_scores - top[..., None]), 0.0)
    denominator = lax.optimization_barrier(jnp.sum(code_weights * cache_counts[:, None, None, :], axis=-1)) + lax.optimization_barrier(jnp.sum(prev_weights, axis=-1)) + lax.optimization_barrier(jnp.sum(cur_weights, axis=-1))
    numerator = jnp.einsum('hgtc,hcd->thgd', code_weights.astype(jnp.bfloat16).astype(jnp.float32), cache_values.astype(jnp.float32))
    numerator = numerator + jnp.einsum('hgtj,jhd->thgd', prev_weights.astype(jnp.bfloat16).astype(jnp.float32), prev_values.astype(jnp.float32))
    numerator = numerator + jnp.einsum('hgtj,jhd->thgd', cur_weights.astype(jnp.bfloat16).astype(jnp.float32), cur_values.astype(jnp.float32))
    attended = numerator / jnp.transpose(denominator, (2, 0, 1))[..., None]
    return attended.reshape(attended.shape[0], -1)

def reference(queries, keys, values, assignments, norm_gain):
    group_size = QH // KH
    num_blocks = TOKENS // BLK
    code_ids = jnp.arange(CODES, dtype=jnp.int32)
    key_heads = keys.reshape(TOKENS, KH, DH).transpose(1, 0, 2)

    def head_sums(pair):
        head_keys, head_codes = pair
        member = (head_codes[:, None] == code_ids[None, :]).astype(jnp.bfloat16)
        sums_here = jnp.dot(member.T, head_keys, preferred_element_type=jnp.float32)
        counts_here = lax.optimization_barrier(jnp.sum(member.astype(jnp.float32), axis=0))
        return (sums_here, counts_here)
    key_sums, code_counts = lax.map(head_sums, (key_heads, assignments))
    codes = (key_sums / code_counts[:, :, None]).astype(jnp.bfloat16)
    quantized = jax.vmap(lambda table, picks: jnp.take(table, picks, axis=0))(codes, assignments)
    query_blocks = queries.reshape(num_blocks, BLK, KH, group_size, DH)
    key_blocks = quantized.reshape(KH, num_blocks, BLK, DH).transpose(1, 0, 2, 3)
    value_blocks = values.reshape(num_blocks, BLK, KH, DH)
    code_blocks = assignments.reshape(KH, num_blocks, BLK).transpose(1, 0, 2)

    def step(carry, block):
        done_sums, done_counts, wait_sums, wait_counts, prev_keys, prev_values, has_prev = carry
        query_rows, cur_keys, cur_values, cur_codes = block
        attended = attend_block(query_rows, cur_keys, cur_values, prev_keys, prev_values, done_sums.astype(jnp.bfloat16), done_counts, codes, has_prev)
        mean_square = lax.optimization_barrier(jnp.mean(attended * attended, axis=1))
        normed_rows = (attended * lax.rsqrt(mean_square + 1e-06)[:, None] * norm_gain).astype(jnp.bfloat16)
        member = (cur_codes[:, :, None] == code_ids[None, None, :]).astype(jnp.float32)
        block_sums = jnp.einsum('htc,thd->hcd', member, cur_values.astype(jnp.float32))
        block_counts = lax.optimization_barrier(jnp.sum(member, axis=1))
        carry = (done_sums + wait_sums, done_counts + wait_counts, block_sums, block_counts, cur_keys, cur_values, jnp.asarray(1.0, jnp.float32))
        return (carry, normed_rows)
    zero_sums = jnp.zeros((KH, CODES, DH), jnp.float32)
    zero_counts = jnp.zeros((KH, CODES), jnp.float32)
    start = (zero_sums, zero_counts, zero_sums, zero_counts, jnp.zeros((KH, BLK, DH), jnp.bfloat16), jnp.zeros((BLK, KH, DH), jnp.bfloat16), jnp.asarray(0.0, jnp.float32))
    final, rows = lax.scan(step, start, (query_blocks, key_blocks, value_blocks, code_blocks))
    return rows.reshape(TOKENS, QH * DH)
```

```python
import functools
import math

import jax
import jax.numpy as jnp
from jax import lax
from jax.experimental import pallas as pl
from jax.experimental.pallas import tpu as pltpu
from jax.sharding import PartitionSpec as P

DH = 128
CODES = 512
CHUNK = 128
MASKED = -1e30
F32 = jnp.float32
BF16 = jnp.bfloat16
KEEP = 1.0 / math.sqrt(DH) * math.log2(math.e)


def one_hot(picks, rows, first=0):
    ids = lax.broadcasted_iota(jnp.int32, (rows, picks.shape[1]), 0) + first
    return jnp.where(ids == picks, 1.0, 0.0).astype(BF16)


def high_low(x):
    high = x.astype(BF16)
    return high, (x - high.astype(F32)).astype(BF16)


def sums_kernel(peers, picks_ref, keys_ref, values_ref, out_ref, seen_ref, member, both):
    tokens = keys_ref.shape[0]
    share = CODES // peers
    both[:, :DH] = keys_ref[...]
    both[:, DH:] = values_ref[...]
    for t in range(0, tokens, 512):
        member[:, t : t + 512] = one_hot(picks_ref[:, t : t + 512], CODES)
    sums = jnp.dot(member[...], both[...], preferred_element_type=F32)
    rows = lax.broadcasted_iota(jnp.int32, (seen_ref.shape[0], tokens), 0)
    cols = lax.broadcasted_iota(jnp.int32, (seen_ref.shape[0], tokens), 1)
    before = jnp.where(cols < rows * CHUNK, 1.0, 0.0).astype(BF16)
    seen = lax.dot_general(
        before, member[...], (((1,), (1,)), ((), ())), preferred_element_type=F32
    )
    seen_ref[...] = seen
    high, low = high_low(sums[:, :DH])
    out_ref[:, :share] = high.reshape(peers, share, DH)
    out_ref[:, share : 2 * share] = low.reshape(peers, share, DH)
    out_ref[:, 2 * share : 3 * share] = sums[:, DH:].astype(BF16).reshape(peers, share, DH)
    counts = seen[tokens // CHUNK : tokens // CHUNK + 1]
    upper = jnp.floor(counts * (1.0 / 16.0)) * 16.0
    lower = counts - upper
    pieces = [
        part[:, k : k + DH] for part in (upper, lower) for k in range(0, CODES, DH)
    ]
    counts_rows = jnp.concatenate(pieces, axis=0).astype(BF16)
    out_ref[:, 3 * share :] = jnp.broadcast_to(
        counts_rows[None], (peers, counts_rows.shape[0], DH)
    )


def combine_kernel(peers, here_ref, parts_ref, out_ref, base_ref):
    share = CODES // peers
    here = here_ref[0]
    counts = parts_ref[:, 3 * share :].astype(F32)
    total = jnp.sum(counts, axis=0)
    place = lax.broadcasted_iota(jnp.int32, counts.shape, 0)
    ahead = jnp.sum(jnp.where(place < here, counts, 0.0), axis=0)
    rows = CODES // DH
    base_ref[...] = ahead[:rows] + ahead[rows:]
    total = total[:rows] + total[rows:]
    code = lax.broadcasted_iota(jnp.int32, (share, DH), 0) + here * share
    lane = lax.broadcasted_iota(jnp.int32, (share, DH), 1)
    mine = jnp.zeros((share, DH), F32)
    for r in range(rows):
        mine = mine + jnp.where(code == lane + r * DH, total[r : r + 1], 0.0)
    mine = jnp.sum(mine, axis=1, keepdims=True)
    key_sums = jnp.sum(parts_ref[:, : 2 * share].astype(F32), axis=0)
    codes = ((key_sums[:share] + key_sums[share:]) / mine).astype(BF16)
    run = jnp.zeros((share, DH), F32)
    for peer in range(peers):
        out_ref[peer, :share] = codes
        out_ref[peer, share:] = run.astype(BF16)
        if peer < peers - 1:
            run = run + parts_ref[peer, 2 * share : 3 * share].astype(F32)


def attend_kernel(
    picks_ref,
    queries_ref,
    values_ref,
    table_ref,
    seen_ref,
    base_ref,
    out_ref,
    squares_ref,
    score_side,
    value_side,
    cache,
    base_row,
    eye,
):
    step = pl.program_id(0)
    share = table_ref.shape[1] // 2
    groups = queries_ref.shape[1] // DH
    lane = lax.broadcasted_iota(jnp.int32, (CODES, DH), 1)
    first_half = lane < DH // 2

    @pl.when(step == 0)
    def _():
        codes = table_ref[:, :share].reshape(CODES, DH)
        score_side[:DH, :CODES] = codes.T
        cache[:, :DH] = table_ref[:, share:].reshape(CODES, DH).astype(F32)
        for r in range(CODES // DH):
            row = base_ref[r : r + 1]
            base_row[:, r * DH : (r + 1) * DH] = row
            cache[r * DH : (r + 1) * DH, DH:] = jnp.broadcast_to(row, (DH, DH)).T
        r = lax.broadcasted_iota(jnp.int32, (CHUNK, CHUNK), 0)
        c = lax.broadcasted_iota(jnp.int32, (CHUNK, CHUNK), 1)
        score_side[DH:, CODES:] = jnp.where(c > r, MASKED, 0.0).astype(BF16)
        eye[...] = jnp.where(c == r, 1.0, 0.0).astype(BF16)
        value_side[CODES:, DH:] = jnp.where(first_half[:CHUNK], 1.0, 0.0).astype(BF16)

    member = one_hot(picks_ref[...], CODES)
    local_keys = jnp.dot(score_side[:DH, :CODES], member, preferred_element_type=F32)
    score_side[:DH, CODES:] = local_keys.astype(BF16)
    present = base_row[...] + seen_ref[pl.ds(step, 1)]
    score_side[DH:, :CODES] = jnp.broadcast_to(
        jnp.where(present > 0.0, 0.0, MASKED), (CHUNK, CODES)
    ).astype(BF16)
    counts = cache[:, DH:]
    upper = jnp.floor(counts * (1.0 / 256.0)) * 256.0
    value_side[:CODES, :DH] = cache[:, :DH].astype(BF16)
    value_side[:CODES, DH:] = jnp.where(first_half, upper, counts - upper).astype(BF16)
    value_side[CODES:, :DH] = values_ref[...]
    ones = jnp.ones((CHUNK, DH), BF16)
    cache[...] += jnp.dot(
        member, jnp.concatenate([values_ref[...], ones], axis=1), preferred_element_type=F32
    )

    squares = jnp.zeros((CHUNK, DH), F32)
    for g in range(groups):
        asked = jnp.concatenate([queries_ref[:, g * DH : (g + 1) * DH], eye[...]], axis=1)
        scores = jnp.dot(asked, score_side[...], preferred_element_type=F32)
        top = jnp.max(scores, axis=1, keepdims=True)
        weights = jnp.exp2((scores - top) * KEEP).astype(BF16)
        mixed = jnp.dot(weights, value_side[...], preferred_element_type=F32)
        tally = mixed[:, DH:]
        attended = mixed[:, :DH] / (tally + pltpu.roll(tally, DH // 2, 1))
        out_ref[:, g * DH : (g + 1) * DH] = attended.astype(out_ref.dtype)
        squares = squares + attended * attended
    pair = jnp.concatenate(high_low(squares), axis=1)
    row = lax.dot_general(
        jnp.ones((8, 2 * DH), BF16), pair, (((1,), (1,)), ((), ())), preferred_element_type=F32
    )[0:1]
    for peer in range(squares_ref.shape[0]):
        squares_ref[peer, pl.ds(step, 1)] = row


def norm_kernel(features, attended_ref, squares_ref, gain_ref, out_ref):
    step = pl.program_id(0)
    chunks = attended_ref.shape[0] // CHUNK
    gain = gain_ref[...]
    for k in range(chunks):
        total = jnp.sum(squares_ref[:, pl.ds(step * chunks + k, 1)], axis=0)
        scale = lax.rsqrt(total * (1.0 / features) + 1e-06)
        scale = jnp.broadcast_to(scale, (DH, CHUNK)).T
        for g in range(attended_ref.shape[1] // DH):
            rows, cols = slice(k * CHUNK, (k + 1) * CHUNK), slice(g * DH, (g + 1) * DH)
            out_ref[rows, cols] = (
                attended_ref[rows, cols].astype(F32) * scale * gain[:, cols]
            ).astype(BF16)


def shape(dims, dtype):
    return jax.ShapeDtypeStruct(dims, dtype)


def local(queries, keys, values, assignments, norm_gain):
    peers = lax.axis_size("seq")
    heads = lax.axis_size("head")
    tokens, width = queries.shape
    chunks = tokens // CHUNK
    share = CODES // peers
    params = functools.partial(pltpu.CompilerParams, vmem_limit_bytes=48 * 2**20)
    count_rows = 2 * CODES // DH

    with jax.named_scope("code_sums"):
        parts, seen = pl.pallas_call(
            functools.partial(sums_kernel, peers),
            out_shape=(
                shape((peers, 3 * share + count_rows, DH), BF16),
                shape((2 * chunks, CODES), F32),
            ),
            scratch_shapes=[pltpu.VMEM((CODES, tokens), BF16), pltpu.VMEM((tokens, 2 * DH), BF16)],
            compiler_params=params(),
        )(assignments, keys, values)
    with jax.named_scope("exchange_sums"):
        parts = lax.all_to_all(parts, "seq", 0, 0)
    with jax.named_scope("combine"):
        here = lax.axis_index("seq").astype(jnp.int32).reshape(1)
        table, base = pl.pallas_call(
            functools.partial(combine_kernel, peers),
            out_shape=(
                shape((peers, 2 * share, DH), BF16),
                shape((CODES // DH, DH), F32),
            ),
            in_specs=[
                pl.BlockSpec(memory_space=pltpu.SMEM),
                pl.BlockSpec(memory_space=pltpu.VMEM),
            ],
            compiler_params=params(),
        )(here, parts)
    with jax.named_scope("exchange_codes"):
        table = lax.all_to_all(table, "seq", 0, 0)
    with jax.named_scope("attend"):
        attended, squares = pl.pallas_call(
            attend_kernel,
            grid=(chunks,),
            in_specs=[
                pl.BlockSpec((1, CHUNK), lambda i: (0, i)),
                pl.BlockSpec((CHUNK, width), lambda i: (i, 0)),
                pl.BlockSpec((CHUNK, DH), lambda i: (i, 0)),
                pl.BlockSpec((peers, 2 * share, DH), lambda i: (0, 0, 0)),
                pl.BlockSpec((2 * chunks, CODES), lambda i: (0, 0)),
                pl.BlockSpec((CODES // DH, DH), lambda i: (0, 0)),
            ],
            out_specs=(
                pl.BlockSpec((CHUNK, width), lambda i: (i, 0)),
                pl.BlockSpec((heads, chunks, CHUNK), lambda i: (0, 0, 0)),
            ),
            out_shape=(
                shape((tokens, width), F32),
                shape((heads, chunks, CHUNK), F32),
            ),
            scratch_shapes=[
                pltpu.VMEM((2 * DH, CODES + CHUNK), BF16),
                pltpu.VMEM((CODES + CHUNK, 2 * DH), BF16),
                pltpu.VMEM((CODES, 2 * DH), F32),
                pltpu.VMEM((1, CODES), F32),
                pltpu.VMEM((CHUNK, CHUNK), BF16),
            ],
            compiler_params=params(dimension_semantics=("arbitrary",)),
        )(assignments, queries, values, table, seen, base)
    with jax.named_scope("exchange_squares"):
        squares = lax.all_to_all(squares, "head", 0, 0)
    with jax.named_scope("norm"):
        step = 4 * CHUNK
        return pl.pallas_call(
            functools.partial(norm_kernel, width * heads),
            grid=(tokens // step,),
            in_specs=[
                pl.BlockSpec((step, width), lambda i: (i, 0)),
                pl.BlockSpec((heads, chunks, CHUNK), lambda i: (0, 0, 0)),
                pl.BlockSpec((1, width), lambda i: (0, 0)),
            ],
            out_specs=pl.BlockSpec((step, width), lambda i: (i, 0)),
            out_shape=shape((tokens, width), BF16),
            compiler_params=params(dimension_semantics=("arbitrary",)),
        )(attended, squares, norm_gain.reshape(1, width))


def solution(mesh):
    in_specs = (P("seq", "head"), P("seq", "head"), P("seq", "head"), P("head", "seq"), P("head"))
    return jax.shard_map(
        local, mesh=mesh, in_specs=in_specs, out_specs=P("seq", "head"), check_vma=False
    )
```

```python
import functools
import math

import jax
import jax.numpy as jnp
from jax import lax
from jax.experimental import pallas as pl
from jax.experimental.pallas import tpu as pltpu
from jax.sharding import PartitionSpec as P

DH = 128
CODES = 512
HALF = 128
CHUNK = 2 * HALF
MASKED = -1e30
F32 = jnp.float32
BF16 = jnp.bfloat16
KEEP = 1.0 / math.sqrt(DH) * math.log2(math.e)


def one_hot(picks, rows, first=0):
    ids = lax.broadcasted_iota(jnp.int32, (rows, picks.shape[1]), 0) + first
    return jnp.where(ids == picks, 1.0, 0.0).astype(BF16)


def high_low(x):
    high = x.astype(BF16)
    return high, (x - high.astype(F32)).astype(BF16)


def sums_kernel(
    peers, picks_hbm, keys_hbm, values_hbm, out_ref, seen_ref, member, picks, both, ready
):
    tokens = both.shape[0]
    share = CODES // peers
    copies = (
        pltpu.make_async_copy(picks_hbm, picks, ready.at[0]),
        pltpu.make_async_copy(keys_hbm, both.at[:, :DH], ready.at[1]),
        pltpu.make_async_copy(values_hbm, both.at[:, DH:], ready.at[2]),
    )
    for copy in copies:
        copy.start()
    copies[0].wait()
    for t in range(0, tokens, 512):
        member[:, t : t + 512] = one_hot(picks[:, t : t + 512], CODES)
    copies[1].wait()
    copies[2].wait()
    sums = jnp.dot(member[...], both[...], preferred_element_type=F32)
    rows = lax.broadcasted_iota(jnp.int32, (seen_ref.shape[0], tokens), 0)
    cols = lax.broadcasted_iota(jnp.int32, (seen_ref.shape[0], tokens), 1)
    before = jnp.where(cols < rows * CHUNK, 1.0, 0.0).astype(BF16)
    seen = lax.dot_general(
        before, member[...], (((1,), (1,)), ((), ())), preferred_element_type=F32
    )
    seen_ref[...] = seen
    high, low = high_low(sums[:, :DH])
    out_ref[:, :share] = high.reshape(peers, share, DH)
    out_ref[:, share : 2 * share] = low.reshape(peers, share, DH)
    out_ref[:, 2 * share : 3 * share] = sums[:, DH:].astype(BF16).reshape(peers, share, DH)
    counts = seen[tokens // CHUNK : tokens // CHUNK + 1]
    upper = jnp.floor(counts * (1.0 / 16.0)) * 16.0
    lower = counts - upper
    pieces = [
        part[:, k : k + DH] for part in (upper, lower) for k in range(0, CODES, DH)
    ]
    counts_rows = jnp.concatenate(pieces, axis=0).astype(BF16)
    out_ref[:, 3 * share :] = jnp.broadcast_to(
        counts_rows[None], (peers, counts_rows.shape[0], DH)
    )


def combine_kernel(peers, here_ref, parts_ref, out_ref, base_ref):
    share = CODES // peers
    here = here_ref[0]
    counts = parts_ref[:, 3 * share :].astype(F32)
    total = jnp.sum(counts, axis=0)
    place = lax.broadcasted_iota(jnp.int32, counts.shape, 0)
    ahead = jnp.sum(jnp.where(place < here, counts, 0.0), axis=0)
    rows = CODES // DH
    base_ref[...] = ahead[:rows] + ahead[rows:]
    total = total[:rows] + total[rows:]
    code = lax.broadcasted_iota(jnp.int32, (share, DH), 0) + here * share
    lane = lax.broadcasted_iota(jnp.int32, (share, DH), 1)
    mine = jnp.zeros((share, DH), F32)
    for r in range(rows):
        mine = mine + jnp.where(code == lane + r * DH, total[r : r + 1], 0.0)
    mine = jnp.sum(mine, axis=1, keepdims=True)
    key_sums = jnp.sum(parts_ref[:, : 2 * share].astype(F32), axis=0)
    codes = ((key_sums[:share] + key_sums[share:]) / mine).astype(BF16)
    run = jnp.zeros((share, DH), F32)
    for peer in range(peers):
        out_ref[peer, :share] = codes
        out_ref[peer, share:] = run.astype(BF16)
        if peer < peers - 1:
            run = run + parts_ref[peer, 2 * share : 3 * share].astype(F32)


def prefix_kernel(member_ref, values_ref, out_ref):
    ones = jnp.ones((CHUNK, DH), BF16)
    run = jnp.zeros((CODES, 2 * DH), F32)
    chunks = out_ref.shape[0]
    for i in range(chunks):
        out_ref[i] = run
        if i < chunks - 1:
            rows = slice(i * CHUNK, (i + 1) * CHUNK)
            both = jnp.concatenate([values_ref[rows], ones], axis=1)
            run = run + jnp.dot(member_ref[:, rows], both, preferred_element_type=F32)


def attend_kernel(
    member_ref,
    queries_hbm,
    values_ref,
    table_ref,
    seen_ref,
    base_ref,
    prefix_hbm,
    out_ref,
    squares_ref,
    score_sides,
    value_sides,
    scores,
    weights,
    base,
    squares,
    queries_ref,
    prefix_ref,
    ready,
):
    share = table_ref.shape[1] // 2
    tokens = queries_ref.shape[0]
    groups = queries_ref.shape[1] // DH
    chunks = tokens // CHUNK
    copies = []
    for i in range(chunks):
        rows = slice(i * CHUNK, (i + 1) * CHUNK)
        copies.append(
            (
                pltpu.make_async_copy(queries_hbm.at[rows], queries_ref.at[rows], ready.at[0, i]),
                pltpu.make_async_copy(prefix_hbm.at[i], prefix_ref.at[i], ready.at[1, i]),
            )
        )
        for copy in copies[i]:
            copy.start()
    lane = lax.broadcasted_iota(jnp.int32, (CODES, DH), 1)
    first_half = lane < DH // 2
    r = lax.broadcasted_iota(jnp.int32, (HALF, HALF), 0)
    c = lax.broadcasted_iota(jnp.int32, (HALF, HALF), 1)
    later = jnp.where(c > r, MASKED, 0.0).astype(BF16)
    eye = jnp.where(c == r, 1.0, 0.0).astype(BF16)
    codes_t = table_ref[:, :share].reshape(CODES, DH).T
    base[:, :DH] = table_ref[:, share:].reshape(CODES, DH).astype(F32)
    for k in range(CODES // DH):
        row = base_ref[k : k + 1]
        base[k * DH : (k + 1) * DH, DH:] = jnp.broadcast_to(row, (DH, DH)).T
    base_row = jnp.concatenate([base_ref[k : k + 1] for k in range(CODES // DH)], axis=1)
    for pair in score_sides:
        pair[0][:DH, :CODES] = codes_t
        pair[1][:DH, :CODES] = codes_t
        pair[0][DH:, CODES:] = later
        pair[1][DH:, CODES:] = jnp.concatenate([jnp.zeros_like(later), later], axis=1)
    for side in value_sides:
        side[CODES:, DH:] = jnp.where(first_half[:CHUNK], 1.0, 0.0).astype(BF16)

    def prepare(i):
        early, late = score_sides[i % 2]
        side = value_sides[i % 2]
        rows = slice(i * CHUNK, (i + 1) * CHUNK)
        for copy in copies[i]:
            copy.wait()
        local_keys = jnp.dot(codes_t, member_ref[:, rows], preferred_element_type=F32).astype(BF16)
        early[:DH, CODES:] = local_keys[:, :HALF]
        late[:DH, CODES:] = local_keys
        present = base_row + seen_ref[i : i + 1]
        mask = jnp.broadcast_to(jnp.where(present > 0.0, 0.0, MASKED), (HALF, CODES)).astype(BF16)
        early[DH:, :CODES] = mask
        late[DH:, :CODES] = mask
        cache = base[...] + prefix_ref[i]
        counts = cache[:, DH:]
        upper = jnp.floor(counts * (1.0 / 256.0)) * 256.0
        side[:CODES, :DH] = cache[:, :DH].astype(BF16)
        side[:CODES, DH:] = jnp.where(first_half, upper, counts - upper).astype(BF16)
        side[CODES:, :DH] = values_ref[rows]

    def score(u):
        rows = slice(u * HALF, (u + 1) * HALF)
        asked = jnp.concatenate(
            [
                jnp.concatenate([queries_ref[rows, g * DH : (g + 1) * DH], eye], axis=1)
                for g in range(groups)
            ],
            axis=0,
        )
        side = score_sides[u // 2 % 2][u % 2]
        scores[u % 2][...] = jnp.dot(asked, side[...], preferred_element_type=F32)

    def weigh(u):
        got = scores[u % 2][...]
        top = jnp.max(got, axis=1, keepdims=True)
        weights[u % 2][...] = jnp.exp2((got - top) * KEEP).astype(BF16)

    def mix(u):
        rows = slice(u * HALF, (u + 1) * HALF)
        side = value_sides[u // 2 % 2]
        width = weights[u % 2].shape[1]
        mixed = jnp.dot(weights[u % 2][...], side[:width], preferred_element_type=F32)
        tally = mixed[:, DH:]
        attended = mixed[:, :DH] / (tally + pltpu.roll(tally, DH // 2, 1))
        total = jnp.zeros((HALF, DH), F32)
        for g in range(groups):
            part = attended[g * HALF : (g + 1) * HALF]
            out_ref[rows, g * DH : (g + 1) * DH] = part
            total = total + part * part
        squares[rows, :DH], squares[rows, DH:] = high_low(total)

    units = 2 * chunks
    for t in range(units + 2):
        if 0 <= t - 2:
            mix(t - 2)
        if 0 <= t - 1 < units:
            weigh(t - 1)
        if t < units:
            if t % 2 == 0:
                prepare(t // 2)
            score(t)
    row = lax.dot_general(
        jnp.ones((8, 2 * DH), BF16),
        squares[...],
        (((1,), (1,)), ((), ())),
        preferred_element_type=F32,
    )[0:1]
    lines = jnp.concatenate([row[:, k : k + DH] for k in range(0, tokens, DH)], axis=0)
    squares_ref[...] = jnp.broadcast_to(lines[None], squares_ref.shape)


def norm_kernel(features, attended_ref, squares_ref, gain_ref, out_ref):
    step = pl.program_id(0)
    chunks = attended_ref.shape[0] // HALF
    gain = gain_ref[...]
    for k in range(chunks):
        total = jnp.sum(squares_ref[:, pl.ds(step * chunks + k, 1)], axis=0)
        scale = lax.rsqrt(total * (1.0 / features) + 1e-06)
        scale = jnp.broadcast_to(scale, (DH, HALF)).T
        for g in range(attended_ref.shape[1] // DH):
            rows, cols = slice(k * HALF, (k + 1) * HALF), slice(g * DH, (g + 1) * DH)
            out_ref[rows, cols] = (
                attended_ref[rows, cols].astype(F32) * scale * gain[:, cols]
            ).astype(BF16)


def shape(dims, dtype):
    return jax.ShapeDtypeStruct(dims, dtype)


def in_hbm(x):
    return pltpu.with_memory_space_constraint(x, pltpu.HBM)


def local(queries, keys, values, assignments, norm_gain):
    peers = lax.axis_size("seq")
    heads = lax.axis_size("head")
    tokens, width = queries.shape
    chunks = tokens // CHUNK
    share = CODES // peers
    count_rows = 2 * CODES // DH

    with jax.named_scope("code_sums"):
        parts, seen, member = pl.pallas_call(
            functools.partial(sums_kernel, peers),
            in_specs=[pl.BlockSpec(memory_space=pltpu.HBM)] * 3,
            out_shape=(
                shape((peers, 3 * share + count_rows, DH), BF16),
                shape((2 * chunks, CODES), F32),
                shape((CODES, tokens), BF16),
            ),
            scratch_shapes=[
                pltpu.VMEM((1, tokens), jnp.int32),
                pltpu.VMEM((tokens, 2 * DH), BF16),
                pltpu.SemaphoreType.DMA((3,)),
            ],
            compiler_params=pltpu.CompilerParams(vmem_limit_bytes=12 * 2**20),
        )(in_hbm(assignments), in_hbm(keys), in_hbm(values))
    with jax.named_scope("exchange_sums"):
        parts = lax.all_to_all(parts, "seq", 0, 0)
    with jax.named_scope("combine"):
        here = lax.axis_index("seq").astype(jnp.int32).reshape(1)
        table, base = pl.pallas_call(
            functools.partial(combine_kernel, peers),
            out_shape=(
                shape((peers, 2 * share, DH), BF16),
                shape((CODES // DH, DH), F32),
            ),
            in_specs=[
                pl.BlockSpec(memory_space=pltpu.SMEM),
                pl.BlockSpec(memory_space=pltpu.VMEM),
            ],
            compiler_params=pltpu.CompilerParams(vmem_limit_bytes=8 * 2**20),
        )(here, parts)
    with jax.named_scope("exchange_codes"):
        table = lax.all_to_all(table, "seq", 0, 0)
    with jax.named_scope("prefix"):
        prefix = pl.pallas_call(
            prefix_kernel,
            out_shape=shape((chunks, CODES, 2 * DH), F32),
            compiler_params=pltpu.CompilerParams(vmem_limit_bytes=12 * 2**20),
            cost_estimate=pl.CostEstimate(
                flops=4 * tokens * CODES * DH, bytes_accessed=2**22, transcendentals=0
            ),
        )(member, values)
    with jax.named_scope("attend"):
        groups = width // DH
        attended, squares = pl.pallas_call(
            attend_kernel,
            out_shape=(
                shape((tokens, width), F32),
                shape((heads, tokens // DH, DH), F32),
            ),
            scratch_shapes=[
                [[pltpu.VMEM((2 * DH, CODES + n * HALF), BF16) for n in (1, 2)] for _ in range(2)],
                [pltpu.VMEM((CODES + CHUNK, 2 * DH), BF16) for _ in range(2)],
                [pltpu.VMEM((groups * HALF, CODES + n * HALF), F32) for n in (1, 2)],
                [pltpu.VMEM((groups * HALF, CODES + n * HALF), BF16) for n in (1, 2)],
                pltpu.VMEM((CODES, 2 * DH), F32),
                pltpu.VMEM((tokens, 2 * DH), BF16),
                pltpu.VMEM((tokens, width), BF16),
                pltpu.VMEM((chunks, CODES, 2 * DH), F32),
                pltpu.SemaphoreType.DMA((2, chunks)),
            ],
            in_specs=[
                pl.BlockSpec(memory_space=pltpu.HBM if x in (1, 6) else pltpu.VMEM)
                for x in range(7)
            ],
            compiler_params=pltpu.CompilerParams(vmem_limit_bytes=28 * 2**20),
        )(member, in_hbm(queries), values, table, seen, base, in_hbm(prefix))
    with jax.named_scope("exchange_squares"):
        squares = lax.all_to_all(squares, "head", 0, 0)
    with jax.named_scope("norm"):
        step = 4 * HALF
        return pl.pallas_call(
            functools.partial(norm_kernel, width * heads),
            grid=(tokens // step,),
            in_specs=[
                pl.BlockSpec((step, width), lambda i: (i, 0)),
                pl.BlockSpec((heads, tokens // DH, DH), lambda i: (0, 0, 0)),
                pl.BlockSpec((1, width), lambda i: (0, 0)),
            ],
            out_specs=pl.BlockSpec((step, width), lambda i: (i, 0)),
            out_shape=shape((tokens, width), BF16),
            compiler_params=pltpu.CompilerParams(vmem_limit_bytes=12 * 2**20, dimension_semantics=("arbitrary",)),
        )(attended, squares, norm_gain.reshape(1, width))


def solution(mesh):
    in_specs = (P("seq", "head"), P("seq", "head"), P("seq", "head"), P("head", "seq"), P("head"))
    return jax.shard_map(
        local, mesh=mesh, in_specs=in_specs, out_specs=P("seq", "head"), check_vma=False
    )
```

```python
import functools
import math

import jax
import jax.numpy as jnp
from jax import lax
from jax.experimental import pallas as pl
from jax.experimental.pallas import tpu as pltpu
from jax.sharding import PartitionSpec as P

DH = 128
CODES = 512
CHUNK = 128
PAIR = 2
MASKED = -1e30
F32 = jnp.float32
BF16 = jnp.bfloat16
KEEP = 1.0 / math.sqrt(DH) * math.log2(math.e)


def one_hot(picks, rows, first=0):
    ids = lax.broadcasted_iota(jnp.int32, (rows, picks.shape[1]), 0) + first
    return jnp.where(ids == picks, 1.0, 0.0).astype(BF16)


def high_low(x):
    high = x.astype(BF16)
    return high, (x - high.astype(F32)).astype(BF16)


def sums_kernel(
    peers, picks_hbm, keys_hbm, values_hbm, out_ref, seen_ref, member, picks, both, ready
):
    tokens = both.shape[0]
    share = CODES // peers
    copies = (
        pltpu.make_async_copy(picks_hbm, picks, ready.at[0]),
        pltpu.make_async_copy(keys_hbm, both.at[:, :DH], ready.at[1]),
        pltpu.make_async_copy(values_hbm, both.at[:, DH:], ready.at[2]),
    )
    for copy in copies:
        copy.start()
    copies[0].wait()
    for t in range(0, tokens, 512):
        member[:, t : t + 512] = one_hot(picks[:, t : t + 512], CODES)
    copies[1].wait()
    copies[2].wait()
    sums = jnp.dot(member[...], both[...], preferred_element_type=F32)
    rows = lax.broadcasted_iota(jnp.int32, (seen_ref.shape[0], tokens), 0)
    cols = lax.broadcasted_iota(jnp.int32, (seen_ref.shape[0], tokens), 1)
    before = jnp.where(cols < rows * CHUNK, 1.0, 0.0).astype(BF16)
    seen = lax.dot_general(
        before, member[...], (((1,), (1,)), ((), ())), preferred_element_type=F32
    )
    seen_ref[...] = seen
    high, low = high_low(sums[:, :DH])
    out_ref[:, :share] = high.reshape(peers, share, DH)
    out_ref[:, share : 2 * share] = low.reshape(peers, share, DH)
    out_ref[:, 2 * share : 3 * share] = sums[:, DH:].astype(BF16).reshape(peers, share, DH)
    counts = seen[tokens // CHUNK : tokens // CHUNK + 1]
    upper = jnp.floor(counts * (1.0 / 16.0)) * 16.0
    lower = counts - upper
    pieces = [
        part[:, k : k + DH] for part in (upper, lower) for k in range(0, CODES, DH)
    ]
    counts_rows = jnp.concatenate(pieces, axis=0).astype(BF16)
    out_ref[:, 3 * share :] = jnp.broadcast_to(
        counts_rows[None], (peers, counts_rows.shape[0], DH)
    )


def combine_kernel(peers, here_ref, parts_ref, out_ref, base_ref):
    share = CODES // peers
    here = here_ref[0]
    counts = parts_ref[:, 3 * share :].astype(F32)
    total = jnp.sum(counts, axis=0)
    place = lax.broadcasted_iota(jnp.int32, counts.shape, 0)
    ahead = jnp.sum(jnp.where(place < here, counts, 0.0), axis=0)
    rows = CODES // DH
    base_ref[...] = ahead[:rows] + ahead[rows:]
    total = total[:rows] + total[rows:]
    code = lax.broadcasted_iota(jnp.int32, (share, DH), 0) + here * share
    lane = lax.broadcasted_iota(jnp.int32, (share, DH), 1)
    mine = jnp.zeros((share, DH), F32)
    for r in range(rows):
        mine = mine + jnp.where(code == lane + r * DH, total[r : r + 1], 0.0)
    mine = jnp.sum(mine, axis=1, keepdims=True)
    key_sums = jnp.sum(parts_ref[:, : 2 * share].astype(F32), axis=0)
    codes = ((key_sums[:share] + key_sums[share:]) / mine).astype(BF16)
    run = jnp.zeros((share, DH), F32)
    for peer in range(peers):
        out_ref[peer, :share] = codes
        out_ref[peer, share:] = run.astype(BF16)
        if peer < peers - 1:
            run = run + parts_ref[peer, 2 * share : 3 * share].astype(F32)


def prepare_kernel(member_ref, values_ref, rows_ref, values_t_ref):
    tokens = values_ref.shape[0]
    for k in range(0, tokens, CHUNK):
        rows_ref[k : k + CHUNK] = member_ref[:, k : k + CHUNK].T
        values_t_ref[:, k : k + CHUNK] = values_ref[k : k + CHUNK].T


def attend_kernel(
    queries_hbm,
    rows_hbm,
    values_t_ref,
    table_ref,
    seen_ref,
    base_ref,
    out_ref,
    squares_ref,
    score_sides,
    value_sides,
    scores,
    weights,
    cache,
    counts,
    later,
    queries_ref,
    rows_ref,
    ready,
):
    share = table_ref.shape[1] // 2
    tokens = queries_ref.shape[0]
    groups = queries_ref.shape[1] // DH
    chunks = tokens // CHUNK
    copies = []
    for i in range(chunks):
        rows = slice(i * CHUNK, (i + 1) * CHUNK)
        copies.append(
            (
                pltpu.make_async_copy(queries_hbm.at[rows], queries_ref.at[rows], ready.at[0, i]),
                pltpu.make_async_copy(rows_hbm.at[rows], rows_ref.at[rows], ready.at[1, i]),
            )
        )
        for copy in copies[i]:
            copy.start()
    upper_half = lax.broadcasted_iota(jnp.int32, (16, CODES), 0) < 8
    codes = table_ref[:, :share].reshape(CODES, DH)
    cache[...] = table_ref[:, share:].reshape(CODES, DH).T.astype(F32)
    base_row = jnp.concatenate([base_ref[k : k + 1] for k in range(CODES // DH)], axis=1)
    counts[...] = base_row + seen_ref[:chunks]
    missing = jnp.where(counts[...] > 0.0, 0.0, MASKED)
    missing = jnp.concatenate([missing, jnp.zeros((DH - chunks, CODES), F32)], axis=0)
    for side in score_sides:
        side[:CODES, :DH] = codes
        side[:CODES, DH:] = missing.T.astype(BF16)
        side[CODES:, DH:] = jnp.zeros((CHUNK, DH), BF16)
    for side in value_sides:
        side[DH:, CODES:] = jnp.where(upper_half[:, :CHUNK], 1.0, 0.0).astype(BF16)
    r = lax.broadcasted_iota(jnp.int32, later.shape, 0)
    c = lax.broadcasted_iota(jnp.int32, later.shape, 1)
    later[...] = jnp.where(r > c % CHUNK, MASKED, 0.0)

    def prepare(i):
        score_side, value_side = score_sides[i % 2], value_sides[i % 2]
        rows = slice(i * CHUNK, (i + 1) * CHUNK)
        for copy in copies[i]:
            copy.wait()
        member = rows_ref[rows]
        local_keys = jnp.dot(member, score_side[:CODES, :DH], preferred_element_type=F32)
        score_side[CODES:, :DH] = local_keys.astype(BF16)
        value_side[:DH, :CODES] = cache[...].astype(BF16)
        value_side[:DH, CODES:] = values_t_ref[:, rows]
        upper = jnp.floor(counts[i : i + 1] * (1.0 / 256.0)) * 256.0
        lower = counts[i : i + 1] - upper
        value_side[DH:, :CODES] = jnp.where(upper_half, upper, lower).astype(BF16)
        if i < chunks - 1:
            cache[...] += jnp.dot(values_t_ref[:, rows], member, preferred_element_type=F32)

    per = groups // PAIR
    units = chunks * per

    def place(u):
        i, first = u // per, u % per * PAIR
        return i, slice(i * CHUNK, (i + 1) * CHUNK), range(first, first + PAIR)

    def score(u):
        i, rows, heads = place(u)
        lane = lax.broadcasted_iota(jnp.int32, (CHUNK, DH), 1)
        now = jnp.where(lane == i, 1.0, 0.0).astype(BF16)
        asked = jnp.concatenate(
            [jnp.concatenate([queries_ref[rows, g * DH : (g + 1) * DH], now], axis=1) for g in heads],
            axis=0,
        )
        scores[u % 2][...] = lax.dot_general(
            score_sides[i % 2][...], asked, (((1,), (1,)), ((), ())), preferred_element_type=F32
        )

    def weigh(u):
        far = scores[u % 2][:CODES]
        near = scores[u % 2][CODES:] + later[...]
        top = jnp.maximum(
            jnp.max(far, axis=0, keepdims=True), jnp.max(near, axis=0, keepdims=True)
        )
        weights[u % 2][:CODES] = jnp.exp2((far - top) * KEEP).astype(BF16)
        weights[u % 2][CODES:] = jnp.exp2((near - top) * KEEP).astype(BF16)

    def mix(u):
        i, rows, heads = place(u)
        mixed = jnp.dot(value_sides[i % 2][...], weights[u % 2][...], preferred_element_type=F32)
        tally = mixed[DH : DH + 8] + mixed[DH + 8 :]
        attended = mixed[:DH] * (1.0 / tally)[0:1]
        total = jnp.sum(attended * attended, axis=0, keepdims=True)
        line = total[:, :CHUNK]
        for n, g in enumerate(heads):
            out_ref[rows, g * DH : (g + 1) * DH] = attended[:, n * CHUNK : (n + 1) * CHUNK].T
            if n:
                line = line + total[:, n * CHUNK : (n + 1) * CHUNK]
        if heads[0]:
            line = line + squares_ref[0, i : i + 1]
        if heads[-1] < groups - 1:
            squares_ref[0, i : i + 1] = line
        else:
            for peer in range(squares_ref.shape[0]):
                squares_ref[peer, i : i + 1] = line

    for t in range(units + 2):
        if t < units and t % per == 0:
            prepare(t // per)
        if t < units:
            score(t)
        if 0 <= t - 1 < units:
            weigh(t - 1)
        if 0 <= t - 2:
            mix(t - 2)


def norm_kernel(features, attended_ref, squares_ref, gain_ref, out_hbm, out, ready):
    tokens, width = attended_ref.shape
    total = jnp.sum(squares_ref[...], axis=0)
    scale = lax.rsqrt(total * (1.0 / features) + 1e-06)
    copies = []
    for i in range(tokens // CHUNK):
        rows = slice(i * CHUNK, (i + 1) * CHUNK)
        column = jnp.broadcast_to(scale[i : i + 1], (DH, CHUNK)).T
        for k in range(0, width, DH):
            cols = slice(k, k + DH)
            out[rows, cols] = (attended_ref[rows, cols] * column * gain_ref[:, cols]).astype(BF16)
        copies.append(pltpu.make_async_copy(out.at[rows], out_hbm.at[rows], ready.at[i]))
        copies[i].start()
    for copy in copies:
        copy.wait()


def shape(dims, dtype):
    return jax.ShapeDtypeStruct(dims, dtype)


def in_hbm(x):
    return pltpu.with_memory_space_constraint(x, pltpu.HBM)


def attend(queries, prepared, table, seen, base, heads):
    rows, values_t = prepared
    tokens, width = queries.shape
    chunks = tokens // CHUNK
    keys = CODES + CHUNK
    return pl.pallas_call(
        attend_kernel,
        out_shape=(
            shape((tokens, width), F32),
            shape((heads, chunks, CHUNK), F32),
        ),
        scratch_shapes=[
            [pltpu.VMEM((keys, 2 * DH), BF16) for _ in range(2)],
            [pltpu.VMEM((DH + 16, keys), BF16) for _ in range(2)],
            [pltpu.VMEM((keys, PAIR * CHUNK), F32) for _ in range(2)],
            [pltpu.VMEM((keys, PAIR * CHUNK), BF16) for _ in range(2)],
            pltpu.VMEM((DH, CODES), F32),
            pltpu.VMEM((chunks, CODES), F32),
            pltpu.VMEM((CHUNK, PAIR * CHUNK), F32),
            pltpu.VMEM((tokens, width), BF16),
            pltpu.VMEM((tokens, CODES), BF16),
            pltpu.SemaphoreType.DMA((2, chunks)),
        ],
        in_specs=[
            pl.BlockSpec(memory_space=pltpu.HBM if x < 2 else pltpu.VMEM) for x in range(6)
        ],
        compiler_params=pltpu.CompilerParams(vmem_limit_bytes=20 * 2**20),
    )(in_hbm(queries), in_hbm(rows), values_t, table, seen, base)


def prepare(member, values):
    tokens = values.shape[0]
    return pl.pallas_call(
        prepare_kernel,
        out_shape=(shape((tokens, CODES), BF16), shape((DH, tokens), BF16)),
        compiler_params=pltpu.CompilerParams(vmem_limit_bytes=12 * 2**20),
        cost_estimate=pl.CostEstimate(
            flops=4 * tokens * CODES * DH, bytes_accessed=2**23, transcendentals=0
        ),
    )(member, values)


def local(queries, keys, values, assignments, norm_gain):
    peers = lax.axis_size("seq")
    heads = lax.axis_size("head")
    tokens, width = queries.shape
    chunks = tokens // CHUNK
    share = CODES // peers
    count_rows = 2 * CODES // DH

    with jax.named_scope("code_sums"):
        parts, seen, member = pl.pallas_call(
            functools.partial(sums_kernel, peers),
            in_specs=[pl.BlockSpec(memory_space=pltpu.HBM)] * 3,
            out_shape=(
                shape((peers, 3 * share + count_rows, DH), BF16),
                shape((2 * chunks, CODES), F32),
                shape((CODES, tokens), BF16),
            ),
            scratch_shapes=[
                pltpu.VMEM((1, tokens), jnp.int32),
                pltpu.VMEM((tokens, 2 * DH), BF16),
                pltpu.SemaphoreType.DMA((3,)),
            ],
            compiler_params=pltpu.CompilerParams(vmem_limit_bytes=12 * 2**20),
        )(in_hbm(assignments), in_hbm(keys), in_hbm(values))
    with jax.named_scope("exchange_sums"):
        parts = lax.all_to_all(parts, "seq", 0, 0)
    with jax.named_scope("combine"):
        here = lax.axis_index("seq").astype(jnp.int32).reshape(1)
        table, base = pl.pallas_call(
            functools.partial(combine_kernel, peers),
            out_shape=(
                shape((peers, 2 * share, DH), BF16),
                shape((CODES // DH, DH), F32),
            ),
            in_specs=[
                pl.BlockSpec(memory_space=pltpu.SMEM),
                pl.BlockSpec(memory_space=pltpu.VMEM),
            ],
            compiler_params=pltpu.CompilerParams(vmem_limit_bytes=8 * 2**20),
        )(here, parts)
    with jax.named_scope("exchange_codes"):
        table = lax.all_to_all(table, "seq", 0, 0)
    with jax.named_scope("prepare"):
        prepared = prepare(member, values)
    with jax.named_scope("attend"):
        attended, squares = attend(queries, prepared, table, seen, base, heads)
    with jax.named_scope("exchange_squares"):
        squares = lax.all_to_all(squares, "head", 0, 0)
    with jax.named_scope("norm"):
        return pl.pallas_call(
            functools.partial(norm_kernel, width * heads),
            out_specs=pl.BlockSpec(memory_space=pltpu.HBM),
            out_shape=shape((tokens, width), BF16),
            scratch_shapes=[
                pltpu.VMEM((tokens, width), BF16),
                pltpu.SemaphoreType.DMA((chunks,)),
            ],
            compiler_params=pltpu.CompilerParams(vmem_limit_bytes=12 * 2**20),
        )(attended, squares, norm_gain.reshape(1, width))


def solution(mesh):
    in_specs = (P("seq", "head"), P("seq", "head"), P("seq", "head"), P("head", "seq"), P("head"))
    return jax.shard_map(
        local, mesh=mesh, in_specs=in_specs, out_specs=P("seq", "head"), check_vma=False
    )
```

```python
import functools
import math

import jax
import jax.numpy as jnp
from jax import lax
from jax.experimental import pallas as pl
from jax.experimental.pallas import tpu as pltpu
from jax.sharding import PartitionSpec as P

DH = 128
CODES = 512
CHUNK = 128
PAIR = 2
MASKED = -1e30
F32 = jnp.float32
BF16 = jnp.bfloat16
KEEP = 1.0 / math.sqrt(DH) * math.log2(math.e)


def one_hot(picks, rows, first=0):
    ids = lax.broadcasted_iota(jnp.int32, (rows, picks.shape[1]), 0) + first
    return jnp.where(ids == picks, 1.0, 0.0).astype(BF16)


def high_low(x):
    high = x.astype(BF16)
    return high, (x - high.astype(F32)).astype(BF16)


def sums_kernel(
    peers, picks_hbm, keys_hbm, values_hbm, out_ref, seen_ref, member, picks, both, ready
):
    tokens = both.shape[0]
    share = CODES // peers
    copies = (
        pltpu.make_async_copy(picks_hbm, picks, ready.at[0]),
        pltpu.make_async_copy(keys_hbm, both.at[:, :DH], ready.at[1]),
        pltpu.make_async_copy(values_hbm, both.at[:, DH:], ready.at[2]),
    )
    for copy in copies:
        copy.start()
    copies[0].wait()
    for t in range(0, tokens, 512):
        member[:, t : t + 512] = one_hot(picks[:, t : t + 512], CODES)
    copies[1].wait()
    copies[2].wait()
    sums = jnp.dot(member[...], both[...], preferred_element_type=F32)
    rows = lax.broadcasted_iota(jnp.int32, (seen_ref.shape[0], tokens), 0)
    cols = lax.broadcasted_iota(jnp.int32, (seen_ref.shape[0], tokens), 1)
    before = jnp.where(cols < rows * CHUNK, 1.0, 0.0).astype(BF16)
    seen = lax.dot_general(
        before, member[...], (((1,), (1,)), ((), ())), preferred_element_type=F32
    )
    seen_ref[...] = seen
    high, low = high_low(sums[:, :DH])
    out_ref[:, :share] = high.reshape(peers, share, DH)
    out_ref[:, share : 2 * share] = low.reshape(peers, share, DH)
    out_ref[:, 2 * share : 3 * share] = sums[:, DH:].astype(BF16).reshape(peers, share, DH)
    counts = seen[tokens // CHUNK : tokens // CHUNK + 1]
    upper = jnp.floor(counts * (1.0 / 16.0)) * 16.0
    lower = counts - upper
    pieces = [
        part[:, k : k + DH] for part in (upper, lower) for k in range(0, CODES, DH)
    ]
    counts_rows = jnp.concatenate(pieces, axis=0).astype(BF16)
    out_ref[:, 3 * share :] = jnp.broadcast_to(
        counts_rows[None], (peers, counts_rows.shape[0], DH)
    )


def combine_kernel(peers, here_ref, parts_ref, out_ref, base_ref):
    share = CODES // peers
    here = here_ref[0]
    counts = parts_ref[:, 3 * share :].astype(F32)
    total = jnp.sum(counts, axis=0)
    place = lax.broadcasted_iota(jnp.int32, counts.shape, 0)
    ahead = jnp.sum(jnp.where(place < here, counts, 0.0), axis=0)
    rows = CODES // DH
    base_ref[...] = ahead[:rows] + ahead[rows:]
    total = total[:rows] + total[rows:]
    code = lax.broadcasted_iota(jnp.int32, (share, DH), 0) + here * share
    lane = lax.broadcasted_iota(jnp.int32, (share, DH), 1)
    mine = jnp.zeros((share, DH), F32)
    for r in range(rows):
        mine = mine + jnp.where(code == lane + r * DH, total[r : r + 1], 0.0)
    mine = jnp.sum(mine, axis=1, keepdims=True)
    key_sums = jnp.sum(parts_ref[:, : 2 * share].astype(F32), axis=0)
    codes = ((key_sums[:share] + key_sums[share:]) / mine).astype(BF16)
    run = jnp.zeros((share, DH), F32)
    for peer in range(peers):
        out_ref[peer, :share] = codes
        out_ref[peer, share:] = run.astype(BF16)
        if peer < peers - 1:
            run = run + parts_ref[peer, 2 * share : 3 * share].astype(F32)


def prepare_kernel(member_ref, values_ref, rows_ref, values_t_ref):
    tokens = values_ref.shape[0]
    for k in range(0, tokens, CHUNK):
        rows_ref[k : k + CHUNK] = member_ref[:, k : k + CHUNK].T
        values_t_ref[:, k : k + CHUNK] = values_ref[k : k + CHUNK].T


def attend_kernel(
    queries_hbm,
    rows_hbm,
    values_t_ref,
    table_ref,
    seen_ref,
    base_ref,
    out_ref,
    squares_ref,
    score_sides,
    value_sides,
    scores,
    weights,
    cache,
    counts,
    later,
    queries_ref,
    rows_ref,
    ready,
):
    share = table_ref.shape[1] // 2
    tokens = queries_ref.shape[0]
    groups = queries_ref.shape[1] // DH
    chunks = tokens // CHUNK
    copies = []
    for i in range(chunks):
        rows = slice(i * CHUNK, (i + 1) * CHUNK)
        copies.append(
            (
                pltpu.make_async_copy(queries_hbm.at[rows], queries_ref.at[rows], ready.at[0, i]),
                pltpu.make_async_copy(rows_hbm.at[rows], rows_ref.at[rows], ready.at[1, i]),
            )
        )
        for copy in copies[i]:
            copy.start()
    upper_half = lax.broadcasted_iota(jnp.int32, (16, CODES), 0) < 8
    codes = table_ref[:, :share].reshape(CODES, DH)
    cache[...] = table_ref[:, share:].reshape(CODES, DH).T.astype(F32)
    base_row = jnp.concatenate([base_ref[k : k + 1] for k in range(CODES // DH)], axis=1)
    counts[...] = base_row + seen_ref[:chunks]
    missing = jnp.where(counts[...] > 0.0, 0.0, MASKED)
    missing = jnp.concatenate([missing, jnp.zeros((DH - chunks, CODES), F32)], axis=0)
    for side in score_sides:
        side[:CODES, :DH] = codes
        side[:CODES, DH:] = missing.T.astype(BF16)
        side[CODES:, DH:] = jnp.zeros((CHUNK, DH), BF16)
    for side in value_sides:
        side[DH:, CODES:] = jnp.where(upper_half[:, :CHUNK], 1.0, 0.0).astype(BF16)
    r = lax.broadcasted_iota(jnp.int32, later.shape, 0)
    c = lax.broadcasted_iota(jnp.int32, later.shape, 1)
    later[...] = jnp.where(r > c % CHUNK, MASKED, 0.0)

    def prepare(i):
        score_side, value_side = score_sides[i % 2], value_sides[i % 2]
        rows = slice(i * CHUNK, (i + 1) * CHUNK)
        member = rows_ref[rows]
        local_keys = jnp.dot(member, score_side[:CODES, :DH], preferred_element_type=F32)
        score_side[CODES:, :DH] = local_keys.astype(BF16)
        value_side[:DH, :CODES] = cache[...].astype(BF16)
        value_side[:DH, CODES:] = values_t_ref[:, rows]
        upper = jnp.floor(counts[i : i + 1] * (1.0 / 256.0)) * 256.0
        lower = counts[i : i + 1] - upper
        value_side[DH:, :CODES] = jnp.where(upper_half, upper, lower).astype(BF16)
        if i < chunks - 1:
            cache[...] += jnp.dot(values_t_ref[:, rows], member, preferred_element_type=F32)

    per = groups // PAIR
    units = chunks * per

    def place(u):
        i, first = u // per, u % per * PAIR
        return i, slice(i * CHUNK, (i + 1) * CHUNK), range(first, first + PAIR)

    def score(u):
        i, rows, heads = place(u)
        lane = lax.broadcasted_iota(jnp.int32, (CHUNK, DH), 1)
        now = jnp.where(lane == i, 1.0, 0.0).astype(BF16)
        asked = jnp.concatenate(
            [jnp.concatenate([queries_ref[rows, g * DH : (g + 1) * DH], now], axis=1) for g in heads],
            axis=0,
        )
        scores[u % 2][...] = lax.dot_general(
            score_sides[i % 2][...], asked, (((1,), (1,)), ((), ())), preferred_element_type=F32
        )

    def weigh(u):
        far = scores[u % 2][:CODES]
        near = scores[u % 2][CODES:] + later[...]
        top = jnp.maximum(
            jnp.max(far, axis=0, keepdims=True), jnp.max(near, axis=0, keepdims=True)
        )
        weights[u % 2][:CODES] = jnp.exp2((far - top) * KEEP).astype(BF16)
        weights[u % 2][CODES:] = jnp.exp2((near - top) * KEEP).astype(BF16)

    def mix(u):
        i, rows, heads = place(u)
        mixed = jnp.dot(value_sides[i % 2][...], weights[u % 2][...], preferred_element_type=F32)
        tally = mixed[DH : DH + 8] + mixed[DH + 8 :]
        attended = mixed[:DH] * (1.0 / tally)[0:1]
        total = jnp.sum(attended * attended, axis=0, keepdims=True)
        line = total[:, :CHUNK]
        for n, g in enumerate(heads):
            out_ref[rows, g * DH : (g + 1) * DH] = attended[:, n * CHUNK : (n + 1) * CHUNK].T
            if n:
                line = line + total[:, n * CHUNK : (n + 1) * CHUNK]
        if heads[0]:
            line = line + squares_ref[0, i : i + 1]
        if heads[-1] < groups - 1:
            squares_ref[0, i : i + 1] = line
        else:
            for peer in range(squares_ref.shape[0]):
                squares_ref[peer, i : i + 1] = line

    for pair in copies:
        for copy in pair:
            copy.wait()
    for t in range(units + 2):
        if t < units and t % per == 0:
            prepare(t // per)
        if t < units:
            score(t)
        if 0 <= t - 1 < units:
            weigh(t - 1)
        if 0 <= t - 2:
            mix(t - 2)


def norm_kernel(features, attended_ref, squares_ref, gain_ref, out_hbm, out, ready):
    tokens, width = attended_ref.shape
    total = jnp.sum(squares_ref[...], axis=0)
    scale = lax.rsqrt(total * (1.0 / features) + 1e-06)
    copies = []
    for i in range(tokens // CHUNK):
        rows = slice(i * CHUNK, (i + 1) * CHUNK)
        column = jnp.broadcast_to(scale[i : i + 1], (DH, CHUNK)).T
        for k in range(0, width, DH):
            cols = slice(k, k + DH)
            out[rows, cols] = (attended_ref[rows, cols] * column * gain_ref[:, cols]).astype(BF16)
        copies.append(pltpu.make_async_copy(out.at[rows], out_hbm.at[rows], ready.at[i]))
        copies[i].start()
    for copy in copies:
        copy.wait()


def shape(dims, dtype):
    return jax.ShapeDtypeStruct(dims, dtype)


def in_hbm(x):
    return pltpu.with_memory_space_constraint(x, pltpu.HBM)


def attend(queries, prepared, table, seen, base, heads):
    rows, values_t = prepared
    tokens, width = queries.shape
    chunks = tokens // CHUNK
    keys = CODES + CHUNK
    return pl.pallas_call(
        attend_kernel,
        out_shape=(
            shape((tokens, width), F32),
            shape((heads, chunks, CHUNK), F32),
        ),
        scratch_shapes=[
            [pltpu.VMEM((keys, 2 * DH), BF16) for _ in range(2)],
            [pltpu.VMEM((DH + 16, keys), BF16) for _ in range(2)],
            [pltpu.VMEM((keys, PAIR * CHUNK), F32) for _ in range(2)],
            [pltpu.VMEM((keys, PAIR * CHUNK), BF16) for _ in range(2)],
            pltpu.VMEM((DH, CODES), F32),
            pltpu.VMEM((chunks, CODES), F32),
            pltpu.VMEM((CHUNK, PAIR * CHUNK), F32),
            pltpu.VMEM((tokens, width), BF16),
            pltpu.VMEM((tokens, CODES), BF16),
            pltpu.SemaphoreType.DMA((2, chunks)),
        ],
        in_specs=[
            pl.BlockSpec(memory_space=pltpu.HBM if x < 2 else pltpu.VMEM) for x in range(6)
        ],
        compiler_params=pltpu.CompilerParams(vmem_limit_bytes=20 * 2**20),
    )(in_hbm(queries), in_hbm(rows), values_t, table, seen, base)


def prepare(member, values):
    tokens = values.shape[0]
    return pl.pallas_call(
        prepare_kernel,
        out_shape=(shape((tokens, CODES), BF16), shape((DH, tokens), BF16)),
        compiler_params=pltpu.CompilerParams(vmem_limit_bytes=12 * 2**20),
        cost_estimate=pl.CostEstimate(
            flops=4 * tokens * CODES * DH, bytes_accessed=2**23, transcendentals=0
        ),
    )(member, values)


def local(queries, keys, values, assignments, norm_gain):
    peers = lax.axis_size("seq")
    heads = lax.axis_size("head")
    tokens, width = queries.shape
    chunks = tokens // CHUNK
    share = CODES // peers
    count_rows = 2 * CODES // DH

    with jax.named_scope("code_sums"):
        parts, seen, member = pl.pallas_call(
            functools.partial(sums_kernel, peers),
            in_specs=[pl.BlockSpec(memory_space=pltpu.HBM)] * 3,
            out_shape=(
                shape((peers, 3 * share + count_rows, DH), BF16),
                shape((2 * chunks, CODES), F32),
                shape((CODES, tokens), BF16),
            ),
            scratch_shapes=[
                pltpu.VMEM((1, tokens), jnp.int32),
                pltpu.VMEM((tokens, 2 * DH), BF16),
                pltpu.SemaphoreType.DMA((3,)),
            ],
            compiler_params=pltpu.CompilerParams(vmem_limit_bytes=12 * 2**20),
        )(in_hbm(assignments), in_hbm(keys), in_hbm(values))
    with jax.named_scope("exchange_sums"):
        parts = lax.all_to_all(parts, "seq", 0, 0)
    with jax.named_scope("combine"):
        here = lax.axis_index("seq").astype(jnp.int32).reshape(1)
        table, base = pl.pallas_call(
            functools.partial(combine_kernel, peers),
            out_shape=(
                shape((peers, 2 * share, DH), BF16),
                shape((CODES // DH, DH), F32),
            ),
            in_specs=[
                pl.BlockSpec(memory_space=pltpu.SMEM),
                pl.BlockSpec(memory_space=pltpu.VMEM),
            ],
            compiler_params=pltpu.CompilerParams(vmem_limit_bytes=8 * 2**20),
        )(here, parts)
    with jax.named_scope("exchange_codes"):
        table = lax.all_to_all(table, "seq", 0, 0)
    with jax.named_scope("prepare"):
        prepared = prepare(member, values)
    with jax.named_scope("attend"):
        attended, squares = attend(queries, prepared, table, seen, base, heads)
    with jax.named_scope("exchange_squares"):
        squares = lax.all_to_all(squares, "head", 0, 0)
    with jax.named_scope("norm"):
        return pl.pallas_call(
            functools.partial(norm_kernel, width * heads),
            out_specs=pl.BlockSpec(memory_space=pltpu.HBM),
            out_shape=shape((tokens, width), BF16),
            scratch_shapes=[
                pltpu.VMEM((tokens, width), BF16),
                pltpu.SemaphoreType.DMA((chunks,)),
            ],
            compiler_params=pltpu.CompilerParams(vmem_limit_bytes=12 * 2**20),
        )(attended, squares, norm_gain.reshape(1, width))


def solution(mesh):
    in_specs = (P("seq", "head"), P("seq", "head"), P("seq", "head"), P("head", "seq"), P("head"))
    return jax.shard_map(
        local, mesh=mesh, in_specs=in_specs, out_specs=P("seq", "head"), check_vma=False
    )
```

```python
import functools
import math

import jax
import jax.numpy as jnp
from jax import lax
from jax.experimental import pallas as pl
from jax.experimental.pallas import tpu as pltpu
from jax.sharding import PartitionSpec as P

DH = 128
CODES = 512
CHUNK = 128
PAIR = 2
MASKED = -1e30
F32 = jnp.float32
BF16 = jnp.bfloat16
KEEP = 1.0 / math.sqrt(DH) * math.log2(math.e)


def one_hot(picks, rows, first=0):
    ids = lax.broadcasted_iota(jnp.int32, (rows, picks.shape[1]), 0) + first
    return jnp.where(ids == picks, 1.0, 0.0).astype(BF16)


def high_low(x):
    high = x.astype(BF16)
    return high, (x - high.astype(F32)).astype(BF16)


def sums_kernel(
    peers, picks_hbm, keys_hbm, values_hbm, out_ref, member, picks, both, ready
):
    tokens = both.shape[0]
    share = CODES // peers
    copies = (
        pltpu.make_async_copy(picks_hbm, picks, ready.at[0]),
        pltpu.make_async_copy(keys_hbm, both.at[:, :DH], ready.at[1]),
        pltpu.make_async_copy(values_hbm, both.at[:, DH:], ready.at[2]),
    )
    for copy in copies:
        copy.start()
    copies[0].wait()
    for t in range(0, tokens, 512):
        member[:, t : t + 512] = one_hot(picks[:, t : t + 512], CODES)
    counts = lax.dot_general(
        jnp.ones((16, tokens), BF16),
        member[...],
        (((1,), (1,)), ((), ())),
        preferred_element_type=F32,
    )[0:1]
    upper = jnp.floor(counts * (1.0 / 16.0)) * 16.0
    lower = counts - upper
    pieces = [
        part[:, k : k + DH] for part in (upper, lower) for k in range(0, CODES, DH)
    ]
    counts_rows = jnp.concatenate(pieces, axis=0).astype(BF16)
    out_ref[:, 3 * share :] = jnp.broadcast_to(
        counts_rows[None], (peers, counts_rows.shape[0], DH)
    )
    copies[1].wait()
    copies[2].wait()
    sums = jnp.dot(member[...], both[...], preferred_element_type=F32)
    high, low = high_low(sums[:, :DH])
    out_ref[:, :share] = high.reshape(peers, share, DH)
    out_ref[:, share : 2 * share] = low.reshape(peers, share, DH)
    out_ref[:, 2 * share : 3 * share] = sums[:, DH:].astype(BF16).reshape(peers, share, DH)


def combine_kernel(peers, here_ref, parts_ref, out_ref, base_ref):
    share = CODES // peers
    here = here_ref[0]
    counts = parts_ref[:, 3 * share :].astype(F32)
    total = jnp.sum(counts, axis=0)
    place = lax.broadcasted_iota(jnp.int32, counts.shape, 0)
    ahead = jnp.sum(jnp.where(place < here, counts, 0.0), axis=0)
    rows = CODES // DH
    base_ref[...] = ahead[:rows] + ahead[rows:]
    total = total[:rows] + total[rows:]
    code = lax.broadcasted_iota(jnp.int32, (share, DH), 0) + here * share
    lane = lax.broadcasted_iota(jnp.int32, (share, DH), 1)
    mine = jnp.zeros((share, DH), F32)
    for r in range(rows):
        mine = mine + jnp.where(code == lane + r * DH, total[r : r + 1], 0.0)
    mine = jnp.sum(mine, axis=1, keepdims=True)
    key_sums = jnp.sum(parts_ref[:, : 2 * share].astype(F32), axis=0)
    codes = ((key_sums[:share] + key_sums[share:]) / mine).astype(BF16)
    run = jnp.zeros((share, DH), F32)
    for peer in range(peers):
        out_ref[peer, :share] = codes
        out_ref[peer, share:] = run.astype(BF16)
        if peer < peers - 1:
            run = run + parts_ref[peer, 2 * share : 3 * share].astype(F32)


def prepare_kernel(
    member_ref, values_ref, base_ref, rows_ref, values_t_ref, missing_ref, counts_ref
):
    tokens = values_ref.shape[0]
    chunks = tokens // CHUNK
    for k in range(0, tokens, CHUNK):
        rows_ref[k : k + CHUNK] = member_ref[:, k : k + CHUNK].T
        values_t_ref[:, k : k + CHUNK] = values_ref[k : k + CHUNK].T
    base_row = jnp.concatenate([base_ref[k : k + 1] for k in range(CODES // DH)], axis=1)
    rows = lax.broadcasted_iota(jnp.int32, (chunks, tokens), 0)
    cols = lax.broadcasted_iota(jnp.int32, (chunks, tokens), 1)
    before = jnp.where(cols < rows * CHUNK, 1.0, 0.0).astype(BF16)
    counts = base_row + lax.dot_general(
        before, member_ref[...], (((1,), (1,)), ((), ())), preferred_element_type=F32
    )
    counts_ref[...] = counts
    missing = jnp.where(counts > 0.0, 0.0, MASKED)
    missing = jnp.concatenate([missing, jnp.zeros((DH - chunks, CODES), F32)], axis=0)
    missing_ref[...] = missing.T.astype(BF16)


def attend_kernel(
    queries_hbm,
    rows_hbm,
    values_t_ref,
    table_ref,
    missing_ref,
    counts_hbm,
    out_ref,
    squares_ref,
    score_sides,
    value_sides,
    scores,
    weights,
    cache,
    later,
    queries_ref,
    rows_ref,
    counts_ref,
    ready,
):
    share = table_ref.shape[1] // 2
    tokens = queries_ref.shape[0]
    groups = queries_ref.shape[1] // DH
    chunks = tokens // CHUNK
    tally_copy = pltpu.make_async_copy(counts_hbm, counts_ref, ready.at[0, chunks])
    tally_copy.start()
    copies = []
    for i in range(chunks):
        rows = slice(i * CHUNK, (i + 1) * CHUNK)
        copies.append(
            (
                pltpu.make_async_copy(queries_hbm.at[rows], queries_ref.at[rows], ready.at[0, i]),
                pltpu.make_async_copy(rows_hbm.at[rows], rows_ref.at[rows], ready.at[1, i]),
            )
        )
        for copy in copies[i]:
            copy.start()
    upper_half = lax.broadcasted_iota(jnp.int32, (16, CODES), 0) < 8
    codes = table_ref[:, :share].reshape(CODES, DH)
    cache[...] = table_ref[:, share:].reshape(CODES, DH).T.astype(F32)
    for side in score_sides:
        side[:CODES, :DH] = codes
        side[:CODES, DH:] = missing_ref[...]
        side[CODES:, DH:] = jnp.zeros((CHUNK, DH), BF16)
    for side in value_sides:
        side[DH:, CODES:] = jnp.where(upper_half[:, :CHUNK], 1.0, 0.0).astype(BF16)
    r = lax.broadcasted_iota(jnp.int32, later.shape, 0)
    c = lax.broadcasted_iota(jnp.int32, later.shape, 1)
    later[...] = jnp.where(r > c % CHUNK, MASKED, 0.0)

    def prepare(i):
        score_side, value_side = score_sides[i % 2], value_sides[i % 2]
        rows = slice(i * CHUNK, (i + 1) * CHUNK)
        member = rows_ref[rows]
        local_keys = jnp.dot(member, score_side[:CODES, :DH], preferred_element_type=F32)
        score_side[CODES:, :DH] = local_keys.astype(BF16)
        value_side[:DH, :CODES] = cache[...].astype(BF16)
        value_side[:DH, CODES:] = values_t_ref[:, rows]
        upper = jnp.floor(counts_ref[i : i + 1] * (1.0 / 256.0)) * 256.0
        lower = counts_ref[i : i + 1] - upper
        value_side[DH:, :CODES] = jnp.where(upper_half, upper, lower).astype(BF16)
        if i < chunks - 1:
            cache[...] += jnp.dot(values_t_ref[:, rows], member, preferred_element_type=F32)

    per = groups // PAIR
    units = chunks * per

    def place(u):
        i, first = u // per, u % per * PAIR
        return i, slice(i * CHUNK, (i + 1) * CHUNK), range(first, first + PAIR)

    def score(u):
        i, rows, heads = place(u)
        lane = lax.broadcasted_iota(jnp.int32, (CHUNK, DH), 1)
        now = jnp.where(lane == i, 1.0, 0.0).astype(BF16)
        asked = jnp.concatenate(
            [jnp.concatenate([queries_ref[rows, g * DH : (g + 1) * DH], now], axis=1) for g in heads],
            axis=0,
        )
        scores[u % 2][...] = lax.dot_general(
            score_sides[i % 2][...], asked, (((1,), (1,)), ((), ())), preferred_element_type=F32
        )

    def weigh(u):
        far = scores[u % 2][:CODES]
        near = scores[u % 2][CODES:] + later[...]
        top = jnp.maximum(
            jnp.max(far, axis=0, keepdims=True), jnp.max(near, axis=0, keepdims=True)
        )
        weights[u % 2][:CODES] = jnp.exp2((far - top) * KEEP).astype(BF16)
        weights[u % 2][CODES:] = jnp.exp2((near - top) * KEEP).astype(BF16)

    def mix(u):
        i, rows, heads = place(u)
        mixed = jnp.dot(value_sides[i % 2][...], weights[u % 2][...], preferred_element_type=F32)
        tally = mixed[DH : DH + 8] + mixed[DH + 8 :]
        attended = mixed[:DH] * (1.0 / tally)[0:1]
        total = jnp.sum(attended * attended, axis=0, keepdims=True)
        line = total[:, :CHUNK]
        for n, g in enumerate(heads):
            out_ref[rows, g * DH : (g + 1) * DH] = attended[:, n * CHUNK : (n + 1) * CHUNK].T
            if n:
                line = line + total[:, n * CHUNK : (n + 1) * CHUNK]
        if heads[0]:
            line = line + squares_ref[0, i : i + 1]
        if heads[-1] < groups - 1:
            squares_ref[0, i : i + 1] = line
        else:
            for peer in range(squares_ref.shape[0]):
                squares_ref[peer, i : i + 1] = line

    tally_copy.wait()
    for pair in copies:
        for copy in pair:
            copy.wait()
    for t in range(units + 2):
        if t < units and t % per == 0:
            prepare(t // per)
        if t < units:
            score(t)
        if 0 <= t - 1 < units:
            weigh(t - 1)
        if 0 <= t - 2:
            mix(t - 2)


def norm_kernel(features, attended_ref, squares_ref, gain_ref, out_hbm, out, ready):
    tokens, width = attended_ref.shape
    total = jnp.sum(squares_ref[...], axis=0)
    scale = lax.rsqrt(total * (1.0 / features) + 1e-06)
    copies = []
    for i in range(tokens // CHUNK):
        rows = slice(i * CHUNK, (i + 1) * CHUNK)
        column = jnp.broadcast_to(scale[i : i + 1], (DH, CHUNK)).T
        for k in range(0, width, DH):
            cols = slice(k, k + DH)
            out[rows, cols] = (attended_ref[rows, cols] * column * gain_ref[:, cols]).astype(BF16)
        copies.append(pltpu.make_async_copy(out.at[rows], out_hbm.at[rows], ready.at[i]))
        copies[i].start()
    for copy in copies:
        copy.wait()


def shape(dims, dtype):
    return jax.ShapeDtypeStruct(dims, dtype)


def in_hbm(x):
    return pltpu.with_memory_space_constraint(x, pltpu.HBM)


def attend(queries, prepared, table, heads):
    rows, values_t, missing, counts = prepared
    tokens, width = queries.shape
    chunks = tokens // CHUNK
    keys = CODES + CHUNK
    return pl.pallas_call(
        attend_kernel,
        out_shape=(
            shape((tokens, width), F32),
            shape((heads, chunks, CHUNK), F32),
        ),
        scratch_shapes=[
            [pltpu.VMEM((keys, 2 * DH), BF16) for _ in range(2)],
            [pltpu.VMEM((DH + 16, keys), BF16) for _ in range(2)],
            [pltpu.VMEM((keys, PAIR * CHUNK), F32) for _ in range(2)],
            [pltpu.VMEM((keys, PAIR * CHUNK), BF16) for _ in range(2)],
            pltpu.VMEM((DH, CODES), F32),
            pltpu.VMEM((CHUNK, PAIR * CHUNK), F32),
            pltpu.VMEM((tokens, width), BF16),
            pltpu.VMEM((tokens, CODES), BF16),
            pltpu.VMEM((chunks, CODES), F32),
            pltpu.SemaphoreType.DMA((2, chunks + 1)),
        ],
        in_specs=[
            pl.BlockSpec(memory_space=pltpu.HBM if x in (0, 1, 5) else pltpu.VMEM) for x in range(6)
        ],
        compiler_params=pltpu.CompilerParams(vmem_limit_bytes=20 * 2**20),
    )(in_hbm(queries), in_hbm(rows), values_t, table, missing, in_hbm(counts))


def prepare(member, values, base):
    tokens = values.shape[0]
    chunks = tokens // CHUNK
    return pl.pallas_call(
        prepare_kernel,
        out_shape=(
            shape((tokens, CODES), BF16),
            shape((DH, tokens), BF16),
            shape((CODES, DH), BF16),
            shape((chunks, CODES), F32),
        ),
        compiler_params=pltpu.CompilerParams(vmem_limit_bytes=12 * 2**20),
        cost_estimate=pl.CostEstimate(
            flops=4 * tokens * CODES * DH, bytes_accessed=2**23, transcendentals=0
        ),
    )(member, values, base)


def local(queries, keys, values, assignments, norm_gain):
    peers = lax.axis_size("seq")
    heads = lax.axis_size("head")
    tokens, width = queries.shape
    chunks = tokens // CHUNK
    share = CODES // peers
    count_rows = 2 * CODES // DH

    with jax.named_scope("code_sums"):
        parts, member = pl.pallas_call(
            functools.partial(sums_kernel, peers),
            in_specs=[pl.BlockSpec(memory_space=pltpu.HBM)] * 3,
            out_shape=(
                shape((peers, 3 * share + count_rows, DH), BF16),
                shape((CODES, tokens), BF16),
            ),
            scratch_shapes=[
                pltpu.VMEM((1, tokens), jnp.int32),
                pltpu.VMEM((tokens, 2 * DH), BF16),
                pltpu.SemaphoreType.DMA((3,)),
            ],
            compiler_params=pltpu.CompilerParams(vmem_limit_bytes=12 * 2**20),
        )(in_hbm(assignments), in_hbm(keys), in_hbm(values))
    with jax.named_scope("exchange_sums"):
        parts = lax.all_to_all(parts, "seq", 0, 0)
    with jax.named_scope("combine"):
        here = lax.axis_index("seq").astype(jnp.int32).reshape(1)
        table, base = pl.pallas_call(
            functools.partial(combine_kernel, peers),
            out_shape=(
                shape((peers, 2 * share, DH), BF16),
                shape((CODES // DH, DH), F32),
            ),
            in_specs=[
                pl.BlockSpec(memory_space=pltpu.SMEM),
                pl.BlockSpec(memory_space=pltpu.VMEM),
            ],
            compiler_params=pltpu.CompilerParams(vmem_limit_bytes=8 * 2**20),
        )(here, parts)
    with jax.named_scope("exchange_codes"):
        table = lax.all_to_all(table, "seq", 0, 0)
    with jax.named_scope("prepare"):
        prepared = prepare(member, values, base)
    with jax.named_scope("attend"):
        attended, squares = attend(queries, prepared, table, heads)
    with jax.named_scope("exchange_squares"):
        squares = lax.all_to_all(squares, "head", 0, 0)
    with jax.named_scope("norm"):
        return pl.pallas_call(
            functools.partial(norm_kernel, width * heads),
            out_specs=pl.BlockSpec(memory_space=pltpu.HBM),
            out_shape=shape((tokens, width), BF16),
            scratch_shapes=[
                pltpu.VMEM((tokens, width), BF16),
                pltpu.SemaphoreType.DMA((chunks,)),
            ],
            compiler_params=pltpu.CompilerParams(vmem_limit_bytes=12 * 2**20),
        )(attended, squares, norm_gain.reshape(1, width))


def solution(mesh):
    in_specs = (P("seq", "head"), P("seq", "head"), P("seq", "head"), P("head", "seq"), P("head"))
    return jax.shard_map(
        local, mesh=mesh, in_specs=in_specs, out_specs=P("seq", "head"), check_vma=False
    )
```

```python
import functools
import math

import jax
import jax.numpy as jnp
from jax import lax
from jax.experimental import pallas as pl
from jax.experimental.pallas import tpu as pltpu
from jax.sharding import PartitionSpec as P

DH = 128
CODES = 512
CHUNK = 128
PAIR = 2
MASKED = -1e30
F32 = jnp.float32
BF16 = jnp.bfloat16
KEEP = 1.0 / math.sqrt(DH) * math.log2(math.e)


def one_hot(picks, rows, first=0):
    ids = lax.broadcasted_iota(jnp.int32, (rows, picks.shape[1]), 0) + first
    return jnp.where(ids == picks, 1.0, 0.0).astype(BF16)


def high_low(x):
    high = x.astype(BF16)
    return high, (x - high.astype(F32)).astype(BF16)


def sums_kernel(
    peers, picks_hbm, keys_hbm, values_hbm, out_ref, member, picks, both, ready
):
    tokens = both.shape[0]
    share = CODES // peers
    copies = (
        pltpu.make_async_copy(picks_hbm, picks, ready.at[0]),
        pltpu.make_async_copy(keys_hbm, both.at[:, :DH], ready.at[1]),
        pltpu.make_async_copy(values_hbm, both.at[:, DH:], ready.at[2]),
    )
    for copy in copies:
        copy.start()
    copies[0].wait()
    for t in range(0, tokens, 512):
        member[:, t : t + 512] = one_hot(picks[:, t : t + 512], CODES)
    counts = lax.dot_general(
        jnp.ones((16, tokens), BF16),
        member[...],
        (((1,), (1,)), ((), ())),
        preferred_element_type=F32,
    )[0:1]
    upper = jnp.floor(counts * (1.0 / 16.0)) * 16.0
    lower = counts - upper
    pieces = [
        part[:, k : k + DH] for part in (upper, lower) for k in range(0, CODES, DH)
    ]
    counts_rows = jnp.concatenate(pieces, axis=0).astype(BF16)
    out_ref[:, 3 * share :] = jnp.broadcast_to(
        counts_rows[None], (peers, counts_rows.shape[0], DH)
    )
    copies[1].wait()
    copies[2].wait()
    sums = jnp.dot(member[...], both[...], preferred_element_type=F32)
    high, low = high_low(sums[:, :DH])
    out_ref[:, :share] = high.reshape(peers, share, DH)
    out_ref[:, share : 2 * share] = low.reshape(peers, share, DH)
    out_ref[:, 2 * share : 3 * share] = sums[:, DH:].astype(BF16).reshape(peers, share, DH)


def combine_kernel(peers, here_ref, parts_ref, out_ref, base_ref):
    share = CODES // peers
    here = here_ref[0]
    counts = parts_ref[:, 3 * share :].astype(F32)
    total = jnp.sum(counts, axis=0)
    place = lax.broadcasted_iota(jnp.int32, counts.shape, 0)
    ahead = jnp.sum(jnp.where(place < here, counts, 0.0), axis=0)
    rows = CODES // DH
    base_ref[...] = ahead[:rows] + ahead[rows:]
    total = total[:rows] + total[rows:]
    code = lax.broadcasted_iota(jnp.int32, (share, DH), 0) + here * share
    lane = lax.broadcasted_iota(jnp.int32, (share, DH), 1)
    mine = jnp.zeros((share, DH), F32)
    for r in range(rows):
        mine = mine + jnp.where(code == lane + r * DH, total[r : r + 1], 0.0)
    mine = jnp.sum(mine, axis=1, keepdims=True)
    key_sums = jnp.sum(parts_ref[:, : 2 * share].astype(F32), axis=0)
    codes = ((key_sums[:share] + key_sums[share:]) / mine).astype(BF16)
    run = jnp.zeros((share, DH), F32)
    for peer in range(peers):
        out_ref[peer, :share] = codes
        out_ref[peer, share:] = run.astype(BF16)
        if peer < peers - 1:
            run = run + parts_ref[peer, 2 * share : 3 * share].astype(F32)


def prepare_kernel(
    member_ref, values_ref, base_ref, rows_ref, values_t_ref, missing_ref, counts_ref
):
    tokens = values_ref.shape[0]
    chunks = tokens // CHUNK
    for k in range(0, tokens, CHUNK):
        rows_ref[k : k + CHUNK] = member_ref[:, k : k + CHUNK].T
        values_t_ref[:, k : k + CHUNK] = values_ref[k : k + CHUNK].T
    base_row = jnp.concatenate([base_ref[k : k + 1] for k in range(CODES // DH)], axis=1)
    rows = lax.broadcasted_iota(jnp.int32, (chunks, tokens), 0)
    cols = lax.broadcasted_iota(jnp.int32, (chunks, tokens), 1)
    before = jnp.where(cols < rows * CHUNK, 1.0, 0.0).astype(BF16)
    counts = base_row + lax.dot_general(
        before, member_ref[...], (((1,), (1,)), ((), ())), preferred_element_type=F32
    )
    counts_ref[...] = counts
    missing = jnp.where(counts > 0.0, 0.0, MASKED)
    missing = jnp.concatenate([missing, jnp.zeros((DH - chunks, CODES), F32)], axis=0)
    missing_ref[...] = missing.T.astype(BF16)


def attend_kernel(
    queries_hbm,
    rows_hbm,
    values_t_ref,
    table_ref,
    missing_ref,
    counts_hbm,
    out_ref,
    squares_ref,
    score_sides,
    value_sides,
    scores,
    weights,
    cache,
    later,
    queries_ref,
    rows_ref,
    counts_ref,
    ready,
):
    share = table_ref.shape[1] // 2
    tokens = queries_ref.shape[0]
    groups = queries_ref.shape[1] // DH
    chunks = tokens // CHUNK
    tally_copy = pltpu.make_async_copy(counts_hbm, counts_ref, ready.at[0, chunks])
    tally_copy.start()
    copies = []
    for i in range(chunks):
        rows = slice(i * CHUNK, (i + 1) * CHUNK)
        copies.append(
            (
                pltpu.make_async_copy(queries_hbm.at[rows], queries_ref.at[rows], ready.at[0, i]),
                pltpu.make_async_copy(rows_hbm.at[rows], rows_ref.at[rows], ready.at[1, i]),
            )
        )
        for copy in copies[i]:
            copy.start()
    upper_half = lax.broadcasted_iota(jnp.int32, (16, CODES), 0) < 8
    codes = table_ref[:, :share].reshape(CODES, DH)
    cache[...] = table_ref[:, share:].reshape(CODES, DH).T.astype(F32)
    for side in score_sides:
        side[:CODES, :DH] = codes
        side[:CODES, DH:] = missing_ref[...]
        side[CODES:, DH:] = jnp.zeros((CHUNK, DH), BF16)
    for side in value_sides:
        side[DH:, CODES:] = jnp.where(upper_half[:, :CHUNK], 1.0, 0.0).astype(BF16)
    r = lax.broadcasted_iota(jnp.int32, later.shape, 0)
    c = lax.broadcasted_iota(jnp.int32, later.shape, 1)
    later[...] = jnp.where(r > c % CHUNK, MASKED, 0.0)

    def prepare(i):
        score_side, value_side = score_sides[i % 2], value_sides[i % 2]
        rows = slice(i * CHUNK, (i + 1) * CHUNK)
        member = rows_ref[rows]
        local_keys = jnp.dot(member, score_side[:CODES, :DH], preferred_element_type=F32)
        score_side[CODES:, :DH] = local_keys.astype(BF16)
        value_side[:DH, :CODES] = cache[...].astype(BF16)
        value_side[:DH, CODES:] = values_t_ref[:, rows]
        upper = jnp.floor(counts_ref[i : i + 1] * (1.0 / 256.0)) * 256.0
        lower = counts_ref[i : i + 1] - upper
        value_side[DH:, :CODES] = jnp.where(upper_half, upper, lower).astype(BF16)
        if i < chunks - 1:
            cache[...] += jnp.dot(values_t_ref[:, rows], member, preferred_element_type=F32)

    per = groups // PAIR
    units = chunks * per

    def place(u):
        i, first = u // per, u % per * PAIR
        return i, slice(i * CHUNK, (i + 1) * CHUNK), range(first, first + PAIR)

    def score(u):
        i, rows, heads = place(u)
        lane = lax.broadcasted_iota(jnp.int32, (CHUNK, DH), 1)
        now = jnp.where(lane == i, 1.0, 0.0).astype(BF16)
        asked = jnp.concatenate(
            [jnp.concatenate([queries_ref[rows, g * DH : (g + 1) * DH], now], axis=1) for g in heads],
            axis=0,
        )
        scores[u % 2][...] = lax.dot_general(
            score_sides[i % 2][...], asked, (((1,), (1,)), ((), ())), preferred_element_type=F32
        )

    def weigh(u):
        far = scores[u % 2][:CODES]
        near = scores[u % 2][CODES:] + later[...]
        top = jnp.maximum(
            jnp.max(far, axis=0, keepdims=True), jnp.max(near, axis=0, keepdims=True)
        )
        weights[u % 2][:CODES] = jnp.exp2((far - top) * KEEP).astype(BF16)
        weights[u % 2][CODES:] = jnp.exp2((near - top) * KEEP).astype(BF16)

    def mix(u):
        i, rows, heads = place(u)
        mixed = jnp.dot(value_sides[i % 2][...], weights[u % 2][...], preferred_element_type=F32)
        tally = mixed[DH : DH + 8] + mixed[DH + 8 :]
        attended = mixed[:DH] * (1.0 / tally)[0:1]
        total = jnp.sum(attended * attended, axis=0, keepdims=True)
        line = total[:, :CHUNK]
        for n, g in enumerate(heads):
            out_ref[rows, g * DH : (g + 1) * DH] = attended[:, n * CHUNK : (n + 1) * CHUNK].T
            if n:
                line = line + total[:, n * CHUNK : (n + 1) * CHUNK]
        if heads[0]:
            line = line + squares_ref[0, i : i + 1]
        if heads[-1] < groups - 1:
            squares_ref[0, i : i + 1] = line
        else:
            for peer in range(squares_ref.shape[0]):
                squares_ref[peer, i : i + 1] = line

    tally_copy.wait()
    for t in range(units + 2):
        if t in (0, 2 * per):
            for pair in copies[:2] if t == 0 else copies[2:]:
                for copy in pair:
                    copy.wait()
        if t < units and t % per == 0:
            prepare(t // per)
        if t < units:
            score(t)
        if 0 <= t - 1 < units:
            weigh(t - 1)
        if 0 <= t - 2:
            mix(t - 2)


def norm_kernel(features, attended_ref, squares_ref, gain_ref, out_hbm, out, ready):
    tokens, width = attended_ref.shape
    total = jnp.sum(squares_ref[...], axis=0)
    scale = lax.rsqrt(total * (1.0 / features) + 1e-06)
    copies = []
    for i in range(tokens // CHUNK):
        rows = slice(i * CHUNK, (i + 1) * CHUNK)
        column = jnp.broadcast_to(scale[i : i + 1], (DH, CHUNK)).T
        for k in range(0, width, DH):
            cols = slice(k, k + DH)
            out[rows, cols] = (attended_ref[rows, cols] * column * gain_ref[:, cols]).astype(BF16)
        copies.append(pltpu.make_async_copy(out.at[rows], out_hbm.at[rows], ready.at[i]))
        copies[i].start()
    for copy in copies:
        copy.wait()


def shape(dims, dtype):
    return jax.ShapeDtypeStruct(dims, dtype)


def in_hbm(x):
    return pltpu.with_memory_space_constraint(x, pltpu.HBM)


def attend(queries, prepared, table, heads):
    rows, values_t, missing, counts = prepared
    tokens, width = queries.shape
    chunks = tokens // CHUNK
    keys = CODES + CHUNK
    return pl.pallas_call(
        attend_kernel,
        out_shape=(
            shape((tokens, width), F32),
            shape((heads, chunks, CHUNK), F32),
        ),
        scratch_shapes=[
            [pltpu.VMEM((keys, 2 * DH), BF16) for _ in range(2)],
            [pltpu.VMEM((DH + 16, keys), BF16) for _ in range(2)],
            [pltpu.VMEM((keys, PAIR * CHUNK), F32) for _ in range(2)],
            [pltpu.VMEM((keys, PAIR * CHUNK), BF16) for _ in range(2)],
            pltpu.VMEM((DH, CODES), F32),
            pltpu.VMEM((CHUNK, PAIR * CHUNK), F32),
            pltpu.VMEM((tokens, width), BF16),
            pltpu.VMEM((tokens, CODES), BF16),
            pltpu.VMEM((chunks, CODES), F32),
            pltpu.SemaphoreType.DMA((2, chunks + 1)),
        ],
        in_specs=[
            pl.BlockSpec(memory_space=pltpu.HBM if x in (0, 1, 5) else pltpu.VMEM) for x in range(6)
        ],
        compiler_params=pltpu.CompilerParams(vmem_limit_bytes=20 * 2**20),
    )(in_hbm(queries), in_hbm(rows), values_t, table, missing, in_hbm(counts))


def prepare(member, values, base):
    tokens = values.shape[0]
    chunks = tokens // CHUNK
    return pl.pallas_call(
        prepare_kernel,
        out_shape=(
            shape((tokens, CODES), BF16),
            shape((DH, tokens), BF16),
            shape((CODES, DH), BF16),
            shape((chunks, CODES), F32),
        ),
        compiler_params=pltpu.CompilerParams(vmem_limit_bytes=12 * 2**20),
        cost_estimate=pl.CostEstimate(
            flops=4 * tokens * CODES * DH, bytes_accessed=2**23, transcendentals=0
        ),
    )(member, values, base)


def local(queries, keys, values, assignments, norm_gain):
    peers = lax.axis_size("seq")
    heads = lax.axis_size("head")
    tokens, width = queries.shape
    chunks = tokens // CHUNK
    share = CODES // peers
    count_rows = 2 * CODES // DH

    with jax.named_scope("code_sums"):
        parts, member = pl.pallas_call(
            functools.partial(sums_kernel, peers),
            in_specs=[pl.BlockSpec(memory_space=pltpu.HBM)] * 3,
            out_shape=(
                shape((peers, 3 * share + count_rows, DH), BF16),
                shape((CODES, tokens), BF16),
            ),
            scratch_shapes=[
                pltpu.VMEM((1, tokens), jnp.int32),
                pltpu.VMEM((tokens, 2 * DH), BF16),
                pltpu.SemaphoreType.DMA((3,)),
            ],
            compiler_params=pltpu.CompilerParams(vmem_limit_bytes=12 * 2**20),
        )(in_hbm(assignments), in_hbm(keys), in_hbm(values))
    with jax.named_scope("exchange_sums"):
        parts = lax.all_to_all(parts, "seq", 0, 0)
    with jax.named_scope("combine"):
        here = lax.axis_index("seq").astype(jnp.int32).reshape(1)
        table, base = pl.pallas_call(
            functools.partial(combine_kernel, peers),
            out_shape=(
                shape((peers, 2 * share, DH), BF16),
                shape((CODES // DH, DH), F32),
            ),
            in_specs=[
                pl.BlockSpec(memory_space=pltpu.SMEM),
                pl.BlockSpec(memory_space=pltpu.VMEM),
            ],
            compiler_params=pltpu.CompilerParams(vmem_limit_bytes=8 * 2**20),
        )(here, parts)
    with jax.named_scope("exchange_codes"):
        table = lax.all_to_all(table, "seq", 0, 0)
    with jax.named_scope("prepare"):
        prepared = prepare(member, values, base)
    with jax.named_scope("attend"):
        attended, squares = attend(queries, prepared, table, heads)
    with jax.named_scope("exchange_squares"):
        squares = lax.all_to_all(squares, "head", 0, 0)
    with jax.named_scope("norm"):
        return pl.pallas_call(
            functools.partial(norm_kernel, width * heads),
            out_specs=pl.BlockSpec(memory_space=pltpu.HBM),
            out_shape=shape((tokens, width), BF16),
            scratch_shapes=[
                pltpu.VMEM((tokens, width), BF16),
                pltpu.SemaphoreType.DMA((chunks,)),
            ],
            compiler_params=pltpu.CompilerParams(vmem_limit_bytes=12 * 2**20),
        )(attended, squares, norm_gain.reshape(1, width))


def solution(mesh):
    in_specs = (P("seq", "head"), P("seq", "head"), P("seq", "head"), P("head", "seq"), P("head"))
    return jax.shard_map(
        local, mesh=mesh, in_specs=in_specs, out_specs=P("seq", "head"), check_vma=False
    )
```

```python
import functools
import math

import jax
import jax.numpy as jnp
from jax import lax
from jax.experimental import pallas as pl
from jax.experimental.pallas import tpu as pltpu
from jax.sharding import PartitionSpec as P

DH = 128
CODES = 512
CHUNK = 128
PAIR = 2
MASKED = -1e30
F32 = jnp.float32
BF16 = jnp.bfloat16
KEEP = 1.0 / math.sqrt(DH) * math.log2(math.e)


def one_hot(picks, rows, first=0):
    ids = lax.broadcasted_iota(jnp.int32, (rows, picks.shape[1]), 0) + first
    return jnp.where(ids == picks, 1.0, 0.0).astype(BF16)


def high_low(x):
    high = x.astype(BF16)
    return high, (x - high.astype(F32)).astype(BF16)


def sums_kernel(
    peers, picks_hbm, keys_hbm, values_hbm, out_ref, member, picks, both, ready
):
    tokens = both.shape[0]
    share = CODES // peers
    copies = (
        pltpu.make_async_copy(picks_hbm, picks, ready.at[0]),
        pltpu.make_async_copy(keys_hbm, both.at[:, :DH], ready.at[1]),
        pltpu.make_async_copy(values_hbm, both.at[:, DH:], ready.at[2]),
    )
    for copy in copies:
        copy.start()
    copies[0].wait()
    for t in range(0, tokens, 512):
        member[:, t : t + 512] = one_hot(picks[:, t : t + 512], CODES)
    counts = lax.dot_general(
        jnp.ones((16, tokens), BF16),
        member[...],
        (((1,), (1,)), ((), ())),
        preferred_element_type=F32,
    )[0:1]
    upper = jnp.floor(counts * (1.0 / 16.0)) * 16.0
    lower = counts - upper
    pieces = [
        part[:, k : k + DH] for part in (upper, lower) for k in range(0, CODES, DH)
    ]
    counts_rows = jnp.concatenate(pieces, axis=0).astype(BF16)
    out_ref[:, 3 * share :] = jnp.broadcast_to(
        counts_rows[None], (peers, counts_rows.shape[0], DH)
    )
    copies[1].wait()
    copies[2].wait()
    sums = jnp.dot(member[...], both[...], preferred_element_type=F32)
    high, low = high_low(sums[:, :DH])
    out_ref[:, :share] = high.reshape(peers, share, DH)
    out_ref[:, share : 2 * share] = low.reshape(peers, share, DH)
    out_ref[:, 2 * share : 3 * share] = sums[:, DH:].astype(BF16).reshape(peers, share, DH)


def combine_kernel(peers, here_ref, parts_ref, out_ref, base_ref):
    share = CODES // peers
    here = here_ref[0]
    counts = parts_ref[:, 3 * share :].astype(F32)
    total = jnp.sum(counts, axis=0)
    place = lax.broadcasted_iota(jnp.int32, counts.shape, 0)
    ahead = jnp.sum(jnp.where(place < here, counts, 0.0), axis=0)
    rows = CODES // DH
    base_ref[...] = ahead[:rows] + ahead[rows:]
    total = total[:rows] + total[rows:]
    code = lax.broadcasted_iota(jnp.int32, (share, DH), 0) + here * share
    lane = lax.broadcasted_iota(jnp.int32, (share, DH), 1)
    mine = jnp.zeros((share, DH), F32)
    for r in range(rows):
        mine = mine + jnp.where(code == lane + r * DH, total[r : r + 1], 0.0)
    mine = jnp.sum(mine, axis=1, keepdims=True)
    key_sums = jnp.sum(parts_ref[:, : 2 * share].astype(F32), axis=0)
    codes = ((key_sums[:share] + key_sums[share:]) / mine).astype(BF16)
    run = jnp.zeros((share, DH), F32)
    for peer in range(peers):
        out_ref[peer, :share] = codes
        out_ref[peer, share:] = run.astype(BF16)
        if peer < peers - 1:
            run = run + parts_ref[peer, 2 * share : 3 * share].astype(F32)


def prepare_kernel(
    member_ref, values_ref, base_ref, rows_ref, values_t_ref, missing_ref, counts_ref
):
    tokens = values_ref.shape[0]
    chunks = tokens // CHUNK
    for k in range(0, tokens, CHUNK):
        rows_ref[k : k + CHUNK] = member_ref[:, k : k + CHUNK].T
        values_t_ref[:, k : k + CHUNK] = values_ref[k : k + CHUNK].T
    base_row = jnp.concatenate([base_ref[k : k + 1] for k in range(CODES // DH)], axis=1)
    rows = lax.broadcasted_iota(jnp.int32, (chunks, tokens), 0)
    cols = lax.broadcasted_iota(jnp.int32, (chunks, tokens), 1)
    before = jnp.where(cols < rows * CHUNK, 1.0, 0.0).astype(BF16)
    counts = base_row + lax.dot_general(
        before, member_ref[...], (((1,), (1,)), ((), ())), preferred_element_type=F32
    )
    counts_ref[...] = counts
    missing = jnp.where(counts > 0.0, 0.0, MASKED)
    missing = jnp.concatenate([missing, jnp.zeros((DH - chunks, CODES), F32)], axis=0)
    missing_ref[...] = missing.T.astype(BF16)


def attend_kernel(
    queries_hbm,
    rows_hbm,
    values_t_ref,
    table_ref,
    missing_ref,
    counts_hbm,
    out_ref,
    squares_ref,
    score_sides,
    value_sides,
    scores,
    weights,
    cache,
    later,
    queries_ref,
    rows_ref,
    counts_ref,
    ready,
):
    share = table_ref.shape[1] // 2
    tokens = queries_ref.shape[0]
    groups = queries_ref.shape[1] // DH
    chunks = tokens // CHUNK
    tally_copy = pltpu.make_async_copy(counts_hbm, counts_ref, ready.at[0, chunks])
    tally_copy.start()
    copies = []
    for i in range(chunks):
        rows = slice(i * CHUNK, (i + 1) * CHUNK)
        copies.append(
            (
                pltpu.make_async_copy(queries_hbm.at[rows], queries_ref.at[rows], ready.at[0, i]),
                pltpu.make_async_copy(rows_hbm.at[rows], rows_ref.at[rows], ready.at[1, i]),
            )
        )
        for copy in copies[i]:
            copy.start()
    upper_half = lax.broadcasted_iota(jnp.int32, (16, CODES), 0) < 8
    codes = table_ref[:, :share].reshape(CODES, DH)
    cache[...] = table_ref[:, share:].reshape(CODES, DH).T.astype(F32)
    for side in score_sides:
        side[:CODES, :DH] = codes
        side[:CODES, DH:] = missing_ref[...]
        side[CODES:, DH:] = jnp.zeros((CHUNK, DH), BF16)
    for side in value_sides:
        side[DH:, CODES:] = jnp.where(upper_half[:, :CHUNK], 1.0, 0.0).astype(BF16)
    r = lax.broadcasted_iota(jnp.int32, later.shape, 0)
    c = lax.broadcasted_iota(jnp.int32, later.shape, 1)
    later[...] = jnp.where(r > c % CHUNK, MASKED, 0.0)

    def prepare(i):
        score_side, value_side = score_sides[i % 2], value_sides[i % 2]
        rows = slice(i * CHUNK, (i + 1) * CHUNK)
        member = rows_ref[rows]
        local_keys = jnp.dot(member, score_side[:CODES, :DH], preferred_element_type=F32)
        score_side[CODES:, :DH] = local_keys.astype(BF16)
        value_side[:DH, :CODES] = cache[...].astype(BF16)
        value_side[:DH, CODES:] = values_t_ref[:, rows]
        upper = jnp.floor(counts_ref[i : i + 1] * (1.0 / 256.0)) * 256.0
        lower = counts_ref[i : i + 1] - upper
        value_side[DH:, :CODES] = jnp.where(upper_half, upper, lower).astype(BF16)
        if i < chunks - 1:
            cache[...] += jnp.dot(values_t_ref[:, rows], member, preferred_element_type=F32)

    per = groups // PAIR
    units = chunks * per

    def place(u):
        i, first = u // per, u % per * PAIR
        return i, slice(i * CHUNK, (i + 1) * CHUNK), range(first, first + PAIR)

    def score(u):
        i, rows, heads = place(u)
        lane = lax.broadcasted_iota(jnp.int32, (CHUNK, DH), 1)
        now = jnp.where(lane == i, 1.0, 0.0).astype(BF16)
        asked = jnp.concatenate(
            [jnp.concatenate([queries_ref[rows, g * DH : (g + 1) * DH], now], axis=1) for g in heads],
            axis=0,
        )
        scores[u % 2][...] = lax.dot_general(
            score_sides[i % 2][...], asked, (((1,), (1,)), ((), ())), preferred_element_type=F32
        )

    def weigh(u):
        far = scores[u % 2][:CODES]
        near = scores[u % 2][CODES:] + later[...]
        top = jnp.maximum(
            jnp.max(far, axis=0, keepdims=True), jnp.max(near, axis=0, keepdims=True)
        )
        weights[u % 2][:CODES] = jnp.exp2((far - top) * KEEP).astype(BF16)
        weights[u % 2][CODES:] = jnp.exp2((near - top) * KEEP).astype(BF16)

    def mix(u):
        i, rows, heads = place(u)
        mixed = jnp.dot(value_sides[i % 2][...], weights[u % 2][...], preferred_element_type=F32)
        tally = mixed[DH : DH + 8] + mixed[DH + 8 :]
        attended = mixed[:DH] * (1.0 / tally)[0:1]
        total = jnp.sum(attended * attended, axis=0, keepdims=True)
        line = total[:, :CHUNK]
        for n, g in enumerate(heads):
            out_ref[rows, g * DH : (g + 1) * DH] = attended[:, n * CHUNK : (n + 1) * CHUNK].T
            if n:
                line = line + total[:, n * CHUNK : (n + 1) * CHUNK]
        if heads[0]:
            line = line + squares_ref[0, i : i + 1]
        if heads[-1] < groups - 1:
            squares_ref[0, i : i + 1] = line
        else:
            for peer in range(squares_ref.shape[0]):
                squares_ref[peer, i : i + 1] = line

    tally_copy.wait()
    for t in range(units + 2):
        if t in (0, 2 * per):
            for pair in copies[:2] if t == 0 else copies[2:]:
                for copy in pair:
                    copy.wait()
        if t < units and t % per == 0:
            prepare(t // per)
        if t < units:
            score(t)
        if 0 <= t - 1 < units:
            weigh(t - 1)
        if 0 <= t - 2:
            mix(t - 2)


def norm_kernel(features, attended_ref, squares_ref, gain_ref, out_hbm, out, ready):
    tokens, width = attended_ref.shape
    total = jnp.sum(squares_ref[...], axis=0)
    scale = lax.rsqrt(total * (1.0 / features) + 1e-06)
    copies = []
    for i in range(tokens // CHUNK):
        rows = slice(i * CHUNK, (i + 1) * CHUNK)
        column = jnp.broadcast_to(scale[i : i + 1], (DH, CHUNK)).T
        for k in range(0, width, DH):
            cols = slice(k, k + DH)
            out[rows, cols] = (attended_ref[rows, cols] * column * gain_ref[:, cols]).astype(BF16)
        if i % 4 == 3:
            done = slice((i - 3) * CHUNK, (i + 1) * CHUNK)
            copies.append(pltpu.make_async_copy(out.at[done], out_hbm.at[done], ready.at[i // 4]))
            copies[-1].start()
    for copy in copies:
        copy.wait()


def shape(dims, dtype):
    return jax.ShapeDtypeStruct(dims, dtype)


def in_hbm(x):
    return pltpu.with_memory_space_constraint(x, pltpu.HBM)


def attend(queries, prepared, table, heads):
    rows, values_t, missing, counts = prepared
    tokens, width = queries.shape
    chunks = tokens // CHUNK
    keys = CODES + CHUNK
    return pl.pallas_call(
        attend_kernel,
        out_shape=(
            shape((tokens, width), F32),
            shape((heads, chunks, CHUNK), F32),
        ),
        scratch_shapes=[
            [pltpu.VMEM((keys, 2 * DH), BF16) for _ in range(2)],
            [pltpu.VMEM((DH + 16, keys), BF16) for _ in range(2)],
            [pltpu.VMEM((keys, PAIR * CHUNK), F32) for _ in range(2)],
            [pltpu.VMEM((keys, PAIR * CHUNK), BF16) for _ in range(2)],
            pltpu.VMEM((DH, CODES), F32),
            pltpu.VMEM((CHUNK, PAIR * CHUNK), F32),
            pltpu.VMEM((tokens, width), BF16),
            pltpu.VMEM((tokens, CODES), BF16),
            pltpu.VMEM((chunks, CODES), F32),
            pltpu.SemaphoreType.DMA((2, chunks + 1)),
        ],
        in_specs=[
            pl.BlockSpec(memory_space=pltpu.HBM if x in (0, 1, 5) else pltpu.VMEM) for x in range(6)
        ],
        compiler_params=pltpu.CompilerParams(vmem_limit_bytes=20 * 2**20),
    )(in_hbm(queries), in_hbm(rows), values_t, table, missing, in_hbm(counts))


def prepare(member, values, base):
    tokens = values.shape[0]
    chunks = tokens // CHUNK
    return pl.pallas_call(
        prepare_kernel,
        out_shape=(
            shape((tokens, CODES), BF16),
            shape((DH, tokens), BF16),
            shape((CODES, DH), BF16),
            shape((chunks, CODES), F32),
        ),
        compiler_params=pltpu.CompilerParams(vmem_limit_bytes=12 * 2**20),
        cost_estimate=pl.CostEstimate(
            flops=4 * tokens * CODES * DH, bytes_accessed=2**23, transcendentals=0
        ),
    )(member, values, base)


def local(queries, keys, values, assignments, norm_gain):
    peers = lax.axis_size("seq")
    heads = lax.axis_size("head")
    tokens, width = queries.shape
    chunks = tokens // CHUNK
    share = CODES // peers
    count_rows = 2 * CODES // DH

    with jax.named_scope("code_sums"):
        parts, member = pl.pallas_call(
            functools.partial(sums_kernel, peers),
            in_specs=[pl.BlockSpec(memory_space=pltpu.HBM)] * 3,
            out_shape=(
                shape((peers, 3 * share + count_rows, DH), BF16),
                shape((CODES, tokens), BF16),
            ),
            scratch_shapes=[
                pltpu.VMEM((1, tokens), jnp.int32),
                pltpu.VMEM((tokens, 2 * DH), BF16),
                pltpu.SemaphoreType.DMA((3,)),
            ],
            compiler_params=pltpu.CompilerParams(vmem_limit_bytes=12 * 2**20),
        )(in_hbm(assignments), in_hbm(keys), in_hbm(values))
    with jax.named_scope("exchange_sums"):
        parts = lax.all_to_all(parts, "seq", 0, 0)
    with jax.named_scope("combine"):
        here = lax.axis_index("seq").astype(jnp.int32).reshape(1)
        table, base = pl.pallas_call(
            functools.partial(combine_kernel, peers),
            out_shape=(
                shape((peers, 2 * share, DH), BF16),
                shape((CODES // DH, DH), F32),
            ),
            in_specs=[
                pl.BlockSpec(memory_space=pltpu.SMEM),
                pl.BlockSpec(memory_space=pltpu.VMEM),
            ],
            compiler_params=pltpu.CompilerParams(vmem_limit_bytes=8 * 2**20),
        )(here, parts)
    with jax.named_scope("exchange_codes"):
        table = lax.all_to_all(table, "seq", 0, 0)
    with jax.named_scope("prepare"):
        prepared = prepare(member, values, base)
    with jax.named_scope("attend"):
        attended, squares = attend(queries, prepared, table, heads)
    with jax.named_scope("exchange_squares"):
        squares = lax.all_to_all(squares, "head", 0, 0)
    with jax.named_scope("norm"):
        return pl.pallas_call(
            functools.partial(norm_kernel, width * heads),
            out_specs=pl.BlockSpec(memory_space=pltpu.HBM),
            out_shape=shape((tokens, width), BF16),
            scratch_shapes=[
                pltpu.VMEM((tokens, width), BF16),
                pltpu.SemaphoreType.DMA((chunks // 4,)),
            ],
            compiler_params=pltpu.CompilerParams(vmem_limit_bytes=12 * 2**20),
        )(attended, squares, norm_gain.reshape(1, width))


def solution(mesh):
    in_specs = (P("seq", "head"), P("seq", "head"), P("seq", "head"), P("head", "seq"), P("head"))
    return jax.shard_map(
        local, mesh=mesh, in_specs=in_specs, out_specs=P("seq", "head"), check_vma=False
    )
```
